512 devices in a mesh: lat: 8 (over z_lo, x), lon: 16 (over y, core), head: 4 (over z_hi).
Axes of the slice: x: 4, y: 8, z: 8 (z_hi: 4, z_lo: 2; z = z_hi * 2 + z_lo), core: 2. Of those that a mesh axis runs over, the one named last changes fastest.
Arguments:
- inputs: bfloat16 [2, 48, 192, 512], P(None, 'lat', 'lon'), may hold values from -6 to 6
- cotangent: bfloat16 [2, 48, 192, 512], P(None, 'lat', 'lon'), may hold values from -6 to 6
- qkv_weight: bfloat16 [2, 512, 3, 512], P(None, None, None, 'head'), may hold values from -0.70710678 to 0.70710678
- proj_weight: bfloat16 [2, 512, 512], P(None, None, 'head'), may hold values from -0.25 to 0.25
- up_weight: bfloat16 [2, 512, 2048], P(None, None, 'head'), may hold values from -0.25 to 0.25
- down_weight: bfloat16 [2, 512, 2048], P(None, None, 'head'), may hold values from -0.125 to 0.125
- shift_labels: int32 [48, 192], P('lat', 'lon'), may hold values from 0 to 2
Outputs:
- layer_out: bfloat16 [2, 48, 192, 512], P(None, 'lat', 'lon')
- input_grad: bfloat16 [2, 48, 192, 512], P(None, 'lat', 'lon')
- qkv_grad: float32 [2, 512, 3, 512], P(None, ('lat', 'lon'), None, 'head')
- proj_grad: float32 [2, 512, 512], P(None, ('lat', 'lon'), 'head')
The draws below stay inside these ranges and needn't reach their ends.
All inputs are finite; a program needn't handle non-finite values.
Results may differ from the reference program's by a relative error of at most 0.034.
Values may be sent and summed in bfloat16 or wider, within the bound.
No kernel may reach another device: no remote copies, remote signals or barrier semaphores. Data moves between devices by JAX's collectives and lax.ppermute only.
A program may use at most 64 MiB of HBM per device.

```python
from functools import partial
import jax
import jax.numpy as jnp
from jax import lax

D = 512
FF = 2048
HD = 64
WIN_LEV = 2
WIN_LAT = 6
WIN_LON = 12
LEVELS = 2
NLAT = 48
NLON = 192
TOKENS = 18432
N_HEAD = 4


def draw_qkv_weight(key, part):
    key = jax.random.fold_in(key, 11)
    key_one = jax.random.fold_in(key, 0)
    baseline = jnp.clip(jax.random.normal(key_one, (2, D, 3, D), jnp.float32), -6.0, 6.0) * D ** (-0.5)
    return baseline.astype(jnp.bfloat16)


def place_ends(values, rng, least, largest):
    index_at = [jax.random.randint(jax.random.fold_in(rng, axis), (), 0, length) for axis, length in enumerate(values.shape)]
    longest = values.shape.index(max(values.shape))
    neighbour = index_at[:longest] + [(index_at[longest] + 1) % values.shape[longest]] + index_at[longest + 1:]
    return values.at[tuple(index_at)].set(least).at[tuple(neighbour)].set(largest)


def steps_of(rng, shape, pieces, low, high):
    loudness = 1.0
    for dim, blocks in pieces:
        draws = jax.random.uniform(jax.random.fold_in(jax.random.fold_in(rng, 6), dim), (blocks,), jnp.float32, low / len(pieces), high / len(pieces))
        loudness = loudness * jnp.repeat(jnp.exp(draws), shape[dim] // blocks).reshape((-1,) + (1,) * (len(shape) - 1 - dim))
    return loudness


def scatter_about(own_key, dims, scale, limit, shards=(), held_as=jnp.bfloat16):
    values = scale * jax.random.normal(own_key, dims, jnp.float32)
    if shards:
        values = values * steps_of(own_key, dims, shards, -0.22, 0.18)
    return jnp.clip(values, -limit, limit).astype(held_as)


def setup_inputs(seed: int = 0) -> dict:
    splits = jax.random.split(jax.random.key(seed), 8)
    return {
        "inputs": scatter_about(splits[0], (LEVELS, NLAT, NLON, D), 1.0, 6.0, ((1, 8), (2, 16))),
        "cotangent": scatter_about(splits[1], (LEVELS, NLAT, NLON, D), 1.0, 6.0, ((1, 8), (2, 16))),
        "qkv_weight": draw_qkv_weight(jax.random.fold_in(splits[7], 71), 0),
        "proj_weight": scatter_about(splits[3], (2, D, D), D ** -0.5, 0.25, ((2, 4),)),
        "up_weight": scatter_about(splits[4], (2, D, FF), D ** -0.5, 0.25, ((2, 4),)),
        "down_weight": scatter_about(splits[5], (2, D, FF), FF ** -0.5, 0.125, ((2, 4),)),
        "shift_labels": place_ends(jax.random.randint(splits[6], (NLAT, NLON), 0, 3), jax.random.fold_in(splits[6], 1), 0, 2).astype(jnp.int32),
    }


EPSILON = 1e-05

def norm_rows(values):
    average = lax.optimization_barrier(jnp.mean(values, axis=-1, keepdims=True))
    centred = values - average
    spread = lax.optimization_barrier(jnp.mean(centred * centred, axis=-1, keepdims=True))
    return centred * lax.rsqrt(spread + EPSILON)

def norm_pull(stream, cotangent):
    _, pullback = jax.vjp(norm_rows, stream.astype(jnp.float32))
    return pullback(cotangent)[0]

def gelu_exact(values):
    return jax.nn.gelu(values, approximate=False)

def to_wire(partial_sum):
    return lax.optimization_barrier(partial_sum.astype(jnp.bfloat16)).astype(jnp.float32)

def to_windows(grid_array):
    level_count, lat_rows, lon_cols, channels = grid_array.shape
    blocks = grid_array.reshape(level_count // WIN_LEV, WIN_LEV, lat_rows // WIN_LAT, WIN_LAT, lon_cols // WIN_LON, WIN_LON, channels)
    blocks = blocks.transpose(0, 2, 4, 1, 3, 5, 6)
    return blocks.reshape(-1, WIN_LEV * WIN_LAT * WIN_LON, channels)

def from_windows(blocks, level_count, lat_rows, lon_cols):
    channels = blocks.shape[-1]
    grid_array = blocks.reshape(level_count // WIN_LEV, lat_rows // WIN_LAT, lon_cols // WIN_LON, WIN_LEV, WIN_LAT, WIN_LON, channels)
    grid_array = grid_array.transpose(0, 3, 1, 4, 2, 5, 6)
    return grid_array.reshape(level_count, lat_rows, lon_cols, channels)

def attend(queries, keys_in, values, allowed):
    factor = queries.shape[-1] ** (-0.5)
    scores = jnp.einsum('wqhd,wkhd->whqk', queries.astype(jnp.float32), keys_in.astype(jnp.float32)) * factor
    scores = jnp.where(allowed[:, None], scores, -1e+30)
    highest = lax.optimization_barrier(jnp.max(scores, axis=-1, keepdims=True))
    weights = jnp.exp(scores - highest)
    weights = weights / lax.optimization_barrier(jnp.sum(weights, axis=-1, keepdims=True))
    rounded = lax.optimization_barrier(weights.astype(jnp.bfloat16)).astype(jnp.float32)
    return jnp.einsum('whqk,wkhd->wqhd', rounded, values.astype(jnp.float32))

def attention_map(packed, allowed):
    level_count, lat_rows, lon_cols, triple, head_width = packed.shape
    blocks = to_windows(packed.reshape(level_count, lat_rows, lon_cols, triple * head_width))
    blocks = blocks.reshape(blocks.shape[0], blocks.shape[1], triple, head_width // HD, HD)
    result = attend(blocks[:, :, 0], blocks[:, :, 1], blocks[:, :, 2], allowed)
    result = result.reshape(result.shape[0], result.shape[1], head_width)
    return from_windows(result, level_count, lat_rows, lon_cols)

def allowed_map(region, level_count):
    grid_array = jnp.broadcast_to(region[None, :, :, None], (level_count,) + region.shape + (1,))
    labels = to_windows(grid_array)[:, :, 0]
    return labels[:, :, None] == labels[:, None, :]

def forward_layer(stream, pack_weight, proj_layer, up_layer, down_layer, region, shifted):
    level_count, lat_rows, lon_cols, model_width = stream.shape
    head_width = model_width // N_HEAD
    hidden_width = up_layer.shape[1] // N_HEAD
    token_rows = stream.reshape(-1, model_width)
    normed = norm_rows(token_rows.astype(jnp.float32)).astype(jnp.bfloat16)
    allowed = allowed_map(region, level_count)
    roll_by = (WIN_LAT // 2, WIN_LON // 2)
    summed = jnp.zeros(token_rows.shape, jnp.float32)
    packs = []
    mixes = []
    for group_index in range(N_HEAD):
        columns = slice(group_index * head_width, (group_index + 1) * head_width)
        w_group = pack_weight[:, :, columns].reshape(model_width, 3 * head_width)
        packed = jnp.dot(normed, w_group, preferred_element_type=jnp.float32).astype(jnp.bfloat16)
        packed = packed.reshape(level_count, lat_rows, lon_cols, 3, head_width)
        if shifted:
            packed = jnp.roll(packed, roll_by, axis=(1, 2))
        mixed_out = attention_map(packed, allowed).astype(jnp.bfloat16)
        if shifted:
            mixed_out = jnp.roll(mixed_out, (-roll_by[0], -roll_by[1]), axis=(1, 2))
        mixed_rows = mixed_out.reshape(-1, head_width)
        partial_sum = lax.dot_general(mixed_rows, proj_layer[:, columns], (((1,), (1,)), ((), ())), preferred_element_type=jnp.float32)
        summed = summed + to_wire(partial_sum)
        packs.append(packed)
        mixes.append(mixed_rows)
    middle = (token_rows.astype(jnp.float32) + summed).astype(jnp.bfloat16)
    second = norm_rows(middle.astype(jnp.float32)).astype(jnp.bfloat16)
    summed = jnp.zeros(token_rows.shape, jnp.float32)
    pre_list = []
    for group_index in range(N_HEAD):
        hidden_cols = slice(group_index * hidden_width, (group_index + 1) * hidden_width)
        pre_act = jnp.dot(second, up_layer[:, hidden_cols], preferred_element_type=jnp.float32)
        activated = gelu_exact(pre_act).astype(jnp.bfloat16)
        partial_sum = lax.dot_general(activated, down_layer[:, hidden_cols], (((1,), (1,)), ((), ())), preferred_element_type=jnp.float32)
        summed = summed + to_wire(partial_sum)
        pre_list.append(pre_act)
    final = (middle.astype(jnp.float32) + summed).astype(jnp.bfloat16)
    stored = (token_rows, normed, allowed, packs, mixes, middle, pre_list)
    return (final.reshape(stream.shape), stored)

def backward_layer(stored, gradient, pack_weight, proj_layer, up_layer, down_layer, shifted, grid_shape):
    token_rows, normed, allowed, packs, mixes, middle, pre_list = stored
    level_count, lat_rows, lon_cols, model_width = grid_shape
    head_width = model_width // N_HEAD
    hidden_width = up_layer.shape[1] // N_HEAD
    roll_by = (WIN_LAT // 2, WIN_LON // 2)
    grad_rows = gradient.reshape(-1, model_width)
    summed = jnp.zeros(grad_rows.shape, jnp.float32)
    for group_index in range(N_HEAD):
        hidden_cols = slice(group_index * hidden_width, (group_index + 1) * hidden_width)
        d_act = jnp.dot(grad_rows, down_layer[:, hidden_cols], preferred_element_type=jnp.float32)
        _, pullback = jax.vjp(gelu_exact, pre_list[group_index])
        d_pre = pullback(d_act)[0].astype(jnp.bfloat16)
        partial_sum = lax.dot_general(d_pre, up_layer[:, hidden_cols], (((1,), (1,)), ((), ())), preferred_element_type=jnp.float32)
        summed = summed + to_wire(partial_sum)
    mid_grad = (grad_rows.astype(jnp.float32) + norm_pull(middle, summed)).astype(jnp.bfloat16)
    summed = jnp.zeros(grad_rows.shape, jnp.float32)
    pack_grads = []
    proj_grads = []
    for group_index in range(N_HEAD):
        columns = slice(group_index * head_width, (group_index + 1) * head_width)
        w_group = pack_weight[:, :, columns].reshape(model_width, 3 * head_width)
        d_mixed = jnp.dot(mid_grad, proj_layer[:, columns], preferred_element_type=jnp.float32).astype(jnp.bfloat16)
        proj_grads.append(lax.dot_general(mid_grad, mixes[group_index], (((0,), (0,)), ((), ())), preferred_element_type=jnp.float32))
        d_grid = d_mixed.reshape(level_count, lat_rows, lon_cols, head_width)
        if shifted:
            d_grid = jnp.roll(d_grid, roll_by, axis=(1, 2))
        _, pullback = jax.vjp(partial(attention_map, allowed=allowed), packs[group_index])
        d_pack = pullback(d_grid.astype(jnp.float32))[0]
        if shifted:
            d_pack = jnp.roll(d_pack, (-roll_by[0], -roll_by[1]), axis=(1, 2))
        d_rows = d_pack.reshape(-1, 3 * head_width)
        pack_grads.append(lax.dot_general(normed, d_rows, (((0,), (0,)), ((), ())), preferred_element_type=jnp.float32).reshape(model_width, 3, head_width))
        partial_sum = lax.dot_general(d_rows, w_group, (((1,), (1,)), ((), ())), preferred_element_type=jnp.float32)
        summed = summed + to_wire(partial_sum)
    in_grad = (mid_grad.astype(jnp.float32) + norm_pull(token_rows, summed)).astype(jnp.bfloat16)
    return (in_grad, jnp.concatenate(pack_grads, axis=2), jnp.concatenate(proj_grads, axis=1))

def reference(inputs, cotangent, qkv_weight, proj_weight, up_weight, down_weight, shift_labels):
    level_count, lat_rows, lon_cols, model_width = inputs.shape
    edge_flag = (jnp.arange(lat_rows) < WIN_LAT // 2).astype(jnp.int32)
    regions = (jnp.zeros((lat_rows, lon_cols), jnp.int32), shift_labels * 2 + edge_flag[:, None])
    stream = inputs
    stores = []
    for layer_index in range(2):
        stream, stored = forward_layer(stream, qkv_weight[layer_index], proj_weight[layer_index], up_weight[layer_index], down_weight[layer_index], regions[layer_index], layer_index == 1)
        stores.append(stored)
    gradient = cotangent
    pack_list = [None, None]
    proj_list = [None, None]
    for layer_index in (1, 0):
        gradient, pack_list[layer_index], proj_list[layer_index] = backward_layer(stores[layer_index], gradient, qkv_weight[layer_index], proj_weight[layer_index], up_weight[layer_index], down_weight[layer_index], layer_index == 1, inputs.shape)
    factor = float(TOKENS) ** (-0.5)
    qkv_grad = jnp.stack(pack_list, axis=0) * factor
    proj_grad = jnp.stack(proj_list, axis=0) * factor
    return (stream, gradient.reshape(inputs.shape), qkv_grad, proj_grad)
```

```python
from functools import partial

import jax
import jax.numpy as jnp
import numpy as np
from jax import lax
from jax.experimental import pallas as pl
from jax.experimental.pallas import tpu as pltpu
from jax.sharding import PartitionSpec as P

HD = 64
EPSILON = 1e-05
PARTS = 4
BF = jnp.bfloat16
F32 = jnp.float32


def norm_rows(values):
    average = jnp.mean(values, axis=-1, keepdims=True)
    centred = values - average
    spread = jnp.mean(centred * centred, axis=-1, keepdims=True)
    return centred * lax.rsqrt(spread + EPSILON)


def norm_pull(stream, cotangent):
    stream = stream.astype(F32)
    average = jnp.mean(stream, axis=-1, keepdims=True)
    centred = stream - average
    spread = jnp.mean(centred * centred, axis=-1, keepdims=True)
    inverse = lax.rsqrt(spread + EPSILON)
    unit = centred * inverse
    mean_c = jnp.mean(cotangent, axis=-1, keepdims=True)
    mean_u = jnp.mean(cotangent * unit, axis=-1, keepdims=True)
    return inverse * (cotangent - mean_c - unit * mean_u)


def dot(left, right, left_dim, right_dim):
    return lax.dot_general(
        left, right, (((left_dim,), (right_dim,)), ((), ())), preferred_element_type=F32
    )


def gelu_and_slope(pre):
    cdf = 0.5 * (1.0 + lax.erf(pre * 0.7071067811865476))
    density = jnp.exp(-0.5 * pre * pre) * 0.3989422804014327
    return pre * cdf, cdf + pre * density


def quads(grid):
    channels = grid.shape[-1]
    return (
        grid.reshape(-1, 2, 3, 2, 6, channels).transpose(1, 3, 0, 2, 4, 5).reshape(PARTS, -1, channels)
    )


def unquads(rows):
    channels = rows.shape[-1]
    return (
        rows.reshape(2, 2, -1, 3, 6, channels)
        .transpose(2, 0, 3, 1, 4, 5)
        .reshape(-1, 6, 12, channels)
    )


def joint(sizes, move):
    pairs = []
    for source in np.ndindex(*sizes):
        target = [t % s for t, s in zip(move(*source), sizes)]
        pairs.append((int(np.ravel_multi_index(source, sizes)), int(np.ravel_multi_index(target, sizes))))
    return pairs


def after(value, *others):
    return lax.optimization_barrier((value,) + others)[0]


def send_quads(pieces, sign):
    sizes = (lax.axis_size("lat"), lax.axis_size("lon"))
    out = [pieces[0]]
    for q in (3, 2, 1):
        perm = joint(sizes, lambda a, b: (a + sign * (q // 2), b + sign * (q % 2)))
        out.insert(1, lax.ppermute(pieces[q], ("lat", "lon"), perm))
    return out


def lat_parts():
    lats = lax.axis_size("lat")
    return 2, lats // 2


def fetch_heads(shard, gate=()):
    low, ring = lat_parts()
    sizes = (low * ring, lax.axis_size("head"))
    shard = after(shard, *gate)

    def odd(hops):
        def move(a, h):
            low_now, x = divmod(a, ring)
            return ((1 - low_now) * ring + x, h + (hops if low_now else -hops))

        return joint(sizes, move)

    def even(a, h):
        return (a, h + (1 if a // ring else -1))

    three = lax.ppermute(shard, ("lat", "head"), odd(2))
    two = lax.ppermute(shard, ("lat", "head"), joint(sizes, even))
    one = lax.ppermute(shard, ("lat", "head"), odd(1))
    return one, two, three


def swap_cores(piece):
    size = lax.axis_size("lon")
    return lax.ppermute(piece, "lon", [(i, i ^ 1) for i in range(size)])


def ring_x(own, long_way, gates=((), ())):
    low, ring = lat_parts()
    size = lax.axis_size("lat")

    def pairs(by):
        return [(i, i // ring * ring + (i + by) % ring) for i in range(size)]

    blocks = {0: own}
    for sign, gate in zip((long_way, -long_way), gates):
        if ring > 2 or sign == long_way:
            sent = after(own, *gate)
            blocks[sign % ring] = lax.ppermute(sent, "lat", pairs(sign))
    if ring > 2:
        blocks[2] = lax.ppermute(blocks[long_way % ring], "lat", pairs(long_way))
    return [blocks[s] for s in range(ring)]


def shard_kernel(ring, qkv_ref, proj_ref, up_ref, down_ref, *refs):
    out_refs, sem = refs[:-1], refs[-1]
    rows, half = out_refs[0].shape
    side = lax.axis_index("lon") % 2
    start = pl.multiple_of(lax.axis_index("lat") % ring * rows, rows)
    width, hidden = proj_ref.shape[2], up_ref.shape[2]
    split = half - 4 * width

    def run(views):
        copies = []
        for layer, out_ref in enumerate(out_refs):
            at = 0
            for view in views(layer):
                target = out_ref.at[:, pl.ds(at, view.shape[1])]
                copies.append(pltpu.make_async_copy(view, target, sem.at[len(copies)]))
                at += view.shape[1]
        for copy in copies:
            copy.start()
        for copy in copies:
            copy.wait()

    @pl.when(side == 0)
    def _():
        run(
            lambda layer: [qkv_ref.at[layer, i, pl.ds(start, rows), :] for i in range(3)]
            + [proj_ref.at[layer, pl.ds(start, rows), :], up_ref.at[layer, pl.ds(start, rows), pl.ds(0, split)]]
        )

    @pl.when(side == 1)
    def _():
        run(
            lambda layer: [
                up_ref.at[layer, pl.ds(start, rows), pl.ds(split, hidden - split)],
                down_ref.at[layer, pl.ds(start, rows), :],
            ]
        )


def weight_shards(own):
    ring = lat_parts()[1]
    columns = 4 * own[1].shape[2] + 2 * own[2].shape[2]
    shard = jax.ShapeDtypeStruct((own[1].shape[1] // ring, columns // 2), BF)
    return pl.pallas_call(
        partial(shard_kernel, ring),
        out_shape=[shard] * 2,
        in_specs=hbm_specs(4),
        out_specs=vmem_specs(2),
        scratch_shapes=[pltpu.SemaphoreType.DMA((10,))],
        compiler_params=pltpu.CompilerParams(vmem_limit_bytes=58 * 1024 * 1024),
    )(*own)


def load_weights(layer, piece_refs, own_refs, w_ref, sem):
    ring = len(piece_refs) // 2
    rows, half = piece_refs[0].shape[1:]
    core = lax.axis_index("lon") % 2
    place = lax.axis_index("lat") % ring
    copies = []
    at = 0
    for ref in own_refs:
        views = [ref.at[layer, i] for i in range(3)] if len(ref.shape) == 4 else [ref.at[layer]]
        for view in views:
            copies.append((view, w_ref.at[0, :, pl.ds(at, view.shape[1])]))
            at += view.shape[1]
    for s in range(ring):
        start = pl.multiple_of((place - s + ring) % ring * rows, rows)
        for side, ref in ((core, piece_refs[s]), (1 - core, piece_refs[ring + s])):
            columns = pl.ds(pl.multiple_of(side * half, half), half)
            copies.append((ref, w_ref.at[pl.ds(1, PARTS - 1), pl.ds(start, rows), columns]))
    copies = [pltpu.make_async_copy(s, d, sem.at[i]) for i, (s, d) in enumerate(copies)]
    for copy in copies:
        copy.start()
    return copies


class Weights:
    def __init__(self, ref, ends):
        self.ref = ref
        self.ends = ends

    def get(self, k, which):
        return self.ref[k, :, self.ends[which] : self.ends[which + 1]]

    qkv = lambda self, k: self.get(k, 0)
    proj = lambda self, k: self.get(k, 1)
    up = lambda self, k: self.get(k, 2)
    down = lambda self, k: self.get(k, 3)


def head_parts(packed, a):
    width = packed.shape[1] // 3
    return tuple(packed[:, i * width + a * HD : i * width + (a + 1) * HD] for i in range(3))


def forward(x, weights, allowed, packed_ref, probs_ref, mixed_ref, slope_ref):
    normed = norm_rows(x).astype(BF)
    total = jnp.zeros(x.shape, F32)
    for k in range(PARTS):
        packed = dot(normed, weights.qkv(k), 1, 0).astype(BF)
        packed_ref[k] = packed
        count = packed.shape[1] // (3 * HD)
        outs = []
        for a in range(count):
            queries, keys, values = head_parts(packed, a)
            scores = dot(queries, keys, 1, 1) * HD**-0.5
            if allowed is not None:
                scores = jnp.where(allowed, scores, -1e30)
            exps = jnp.exp(scores - jnp.max(scores, axis=-1, keepdims=True))
            probs = exps / jnp.sum(exps, axis=-1, keepdims=True)
            probs_ref[k * count + a] = probs
            outs.append(dot(probs.astype(BF), values, 1, 0))
        mixed = jnp.concatenate(outs, axis=1).astype(BF)
        if k == 0:
            mixed_ref[...] = mixed
        total += dot(mixed, weights.proj(k), 1, 1)
    middle = (x + total).astype(BF)
    second = norm_rows(middle.astype(F32)).astype(BF)
    total = jnp.zeros(x.shape, F32)
    for k in range(PARTS):
        active, slope = gelu_and_slope(dot(second, weights.up(k), 1, 0))
        slope_ref[k] = slope
        total += dot(active.astype(BF), weights.down(k), 1, 1)
    return middle, (middle.astype(F32) + total).astype(BF)


def backward(x, middle, gradient, weights, factor, packed_ref, probs_ref, mixed_ref, slope_ref, sums_ref):
    middle = middle.astype(F32)
    total = jnp.zeros(x.shape, F32)
    for k in range(PARTS):
        d_pre = (slope_ref[k] * dot(gradient, weights.down(k), 1, 0)).astype(BF)
        total += dot(d_pre, weights.up(k), 1, 1)
    mid_grad = (gradient.astype(F32) + norm_pull(middle, total)).astype(BF)
    total = jnp.zeros(x.shape, F32)
    for k in range(PARTS):
        d_mixed = dot(mid_grad, weights.proj(k), 1, 0).astype(BF)
        packed = packed_ref[k]
        width = d_mixed.shape[1]
        count = width // HD
        parts = [[], [], []]
        for a in range(count):
            queries, keys, values = head_parts(packed, a)
            d_out = d_mixed[:, a * HD : (a + 1) * HD]
            probs = probs_ref[k * count + a]
            d_probs = dot(d_out, values, 1, 1)
            d_scores = probs * (d_probs - jnp.sum(d_probs * probs, axis=-1, keepdims=True))
            d_scores = (d_scores * HD**-0.5).astype(BF)
            parts[0].append(dot(d_scores, keys, 1, 0))
            parts[1].append(dot(d_scores, queries, 0, 0))
            parts[2].append(dot(probs.astype(BF), d_out, 0, 0))
        d_packed = jnp.concatenate(parts[0] + parts[1] + parts[2], axis=1).astype(BF)
        total += dot(d_packed, weights.qkv(k), 1, 1)
        if k == 0:
            normed = norm_rows(x).astype(BF)
            sums_ref[:, : 3 * width] = (dot(normed, d_packed, 0, 0) * factor).astype(BF)
            sums_ref[:, 3 * width :] = (dot(mid_grad, mixed_ref[...], 0, 0) * factor).astype(BF)
    return (mid_grad.astype(F32) + norm_pull(x, total)).astype(BF)


def first_kernel(pieces, ends, *refs):
    x_ref, refs = refs[0], refs[1:]
    piece_refs, own_refs, refs = refs[:pieces], refs[pieces : pieces + 4], refs[pieces + 4 :]
    out_refs, (w_ref, middle_ref, *saved), sem = refs[:PARTS], refs[PARTS:-1], refs[-1]
    copies = load_weights(0, piece_refs, own_refs, w_ref, sem)
    for copy in copies:
        copy.wait()
    middle, out = forward(x_ref[...].astype(F32), Weights(w_ref, ends), None, *saved)
    middle_ref[...] = middle
    rows = out.shape[0] // PARTS
    for q in range(PARTS):
        out_refs[q][...] = out[q * rows : (q + 1) * rows]


def second_kernel(pieces, ends, factor, *refs):
    x_refs, grad_refs, refs = refs[:PARTS], refs[PARTS : 2 * PARTS], refs[2 * PARTS :]
    column_ref, row_ref, *refs = refs
    piece_refs, own_refs, refs = refs[:pieces], refs[pieces : pieces + 4], refs[pieces + 4 :]
    out_refs, (sums_ref, w_ref, *saved), sem = refs[:PARTS], refs[PARTS:-1], refs[-1]
    copies = load_weights(1, piece_refs, own_refs, w_ref, sem)
    x = jnp.concatenate([ref[...].astype(F32) for ref in x_refs], axis=0)
    allowed = column_ref[...] == row_ref[...]
    for copy in copies:
        copy.wait()
    weights = Weights(w_ref, ends)
    middle, out = forward(x, weights, allowed, *saved)
    rows = out.shape[0] // PARTS
    for q in range(PARTS):
        out_refs[q][0] = out[q * rows : (q + 1) * rows]
    gradient = jnp.concatenate([ref[...].astype(F32) for ref in grad_refs], axis=0).astype(BF)
    result = backward(x, middle, gradient, weights, factor, *saved, sums_ref)
    for q in range(PARTS):
        out_refs[q][1] = result[q * rows : (q + 1) * rows]


def third_kernel(ends, factor, *refs):
    grad_refs, (x_ref, w_ref, middle_ref, *saved), (result_ref, sums_ref) = refs[:PARTS], refs[PARTS:-2], refs[-2:]
    gradient = jnp.concatenate([ref[1].astype(F32) for ref in grad_refs], axis=0).astype(BF)
    weights = Weights(w_ref, ends)
    result_ref[...] = backward(
        x_ref[...].astype(F32), middle_ref[...], gradient, weights, factor, *saved, sums_ref
    )


def vmem_specs(count):
    return [pl.BlockSpec(memory_space=pltpu.VMEM)] * count


def any_specs(count):
    return [pl.BlockSpec(memory_space=pl.ANY)] * count


def hbm_specs(count):
    return [pl.BlockSpec(memory_space=pltpu.HBM)] * count


PARAMS = pltpu.CompilerParams(vmem_limit_bytes=28 * 1024 * 1024)


def cost(flops):
    return pl.CostEstimate(flops=flops, bytes_accessed=8_000_000, transcendentals=600_000)


def scatter(parts, axis):
    size = lax.axis_size(axis)
    parts = parts.reshape(size, -1, parts.shape[-1])
    return jnp.sum(lax.all_to_all(parts, axis, 0, 0).astype(F32), axis=0)


def per_device(inputs, cotangent, qkv_weight, proj_weight, up_weight, down_weight, shift_labels):
    level_count, lat_rows, lon_cols, model_width = inputs.shape
    head_width = qkv_weight.shape[-1]
    tokens = level_count * lat_rows * lon_cols
    quarter = tokens // PARTS
    factor = float(tokens * lax.axis_size("lat") * lax.axis_size("lon")) ** -0.5

    own = (qkv_weight.swapaxes(1, 2), proj_weight, up_weight, down_weight)
    ends = [0, 3 * head_width, 4 * head_width]
    ends = ends + [ends[-1] + up_weight.shape[2], ends[-1] + 2 * up_weight.shape[2]]
    shards = weight_shards(own)
    early = fetch_heads(shards[0])
    ending = send_quads(list(after(quads(cotangent), early[0])), 1)
    edge = ((jnp.arange(lat_rows) < 3) & (lax.axis_index("lat") == 0)).astype(jnp.int32)
    region = jnp.broadcast_to((shift_labels * 2 + edge[:, None])[None, :, :, None], (level_count, 6, 12, 1))
    labels = quads(region)[::-1].reshape(-1)
    column, row = labels[:, None], labels[None, :]
    start = quads(inputs).reshape(tokens, model_width)
    early_block, start, column, row, *ending = lax.optimization_barrier(
        (jnp.stack(early), start, column, row, *ending)
    )
    early_ring = ring_x(early_block, 1)
    early_swaps = [swap_cores(early_block)]
    late = fetch_heads(shards[1], early_swaps[:1])
    late_ring = ring_x(jnp.stack(late), -1, (early_ring[1::2], early_ring[2:3]))
    early_swaps += [swap_cores(piece) for piece in early_ring[1:]]
    early_all = early_ring + early_swaps
    late_swaps = {s: swap_cores(late_ring[s]) for s in (0, len(late_ring) - 1)}
    start = after(start, *late_swaps.values())

    width = head_width // HD * PARTS
    stream = jax.ShapeDtypeStruct((tokens, model_width), BF)
    piece = jax.ShapeDtypeStruct((quarter, model_width), BF)
    pair = jax.ShapeDtypeStruct((2, quarter, model_width), BF)
    sums = jax.ShapeDtypeStruct((model_width, 4 * head_width), BF)
    full_weights = jax.ShapeDtypeStruct((PARTS, model_width, ends[-1]), BF)
    saved = [
        jax.ShapeDtypeStruct((PARTS, tokens, 3 * head_width), BF),
        jax.ShapeDtypeStruct((width, tokens, tokens), F32),
        jax.ShapeDtypeStruct((tokens, head_width), BF),
        jax.ShapeDtypeStruct((PARTS, tokens, up_weight.shape[2]), F32),
    ]
    pieces = len(early_all)
    semaphores = pltpu.SemaphoreType.DMA((pieces + 6,))

    *quarters, early_weights, middle, packed, probs, mixed, slope = pl.pallas_call(
        partial(first_kernel, pieces, ends),
        out_shape=[piece] * PARTS + [full_weights, stream] + saved,
        in_specs=vmem_specs(1) + any_specs(pieces) + hbm_specs(4),
        out_specs=vmem_specs(PARTS + 6),
        scratch_shapes=[semaphores],
        compiler_params=PARAMS,
        cost_estimate=cost(1_800_000_000),
    )(start, *early_all, *own)
    quarters = send_quads(quarters, 1)
    for s, piece in enumerate(late_ring):
        if s not in late_swaps:
            late_swaps[s] = swap_cores(after(piece, *quarters[1:]))
    late_all = late_ring + [late_swaps[s] for s in range(len(late_ring))]
    *pairs, late_sum = pl.pallas_call(
        partial(second_kernel, pieces, ends, factor),
        out_shape=[pair] * PARTS + [sums],
        in_specs=vmem_specs(2 * PARTS + 2) + any_specs(pieces) + hbm_specs(4),
        out_specs=vmem_specs(PARTS + 1),
        scratch_shapes=[pltpu.VMEM(s.shape, s.dtype) for s in [full_weights] + saved] + [semaphores],
        compiler_params=PARAMS,
        cost_estimate=cost(3_800_000_000),
    )(*quarters, *ending, column, row, *late_all, *own)
    pairs = send_quads(pairs, -1)
    late_sum = scatter(late_sum, "lat")
    input_grad, early_sum = pl.pallas_call(
        partial(third_kernel, ends, factor),
        out_shape=[stream, sums],
        in_specs=vmem_specs(PARTS + 7),
        out_specs=vmem_specs(2),
        compiler_params=PARAMS,
        cost_estimate=cost(2_000_000_000),
    )(*pairs, start, early_weights, middle, packed, probs, mixed, slope)

    layer_out = unquads(jnp.stack([p[0] for p in pairs]))
    total = jnp.stack([scatter(early_sum, "lat"), late_sum])
    lons = lax.axis_size("lon")
    total = total.astype(BF).reshape(2, lons, -1, 4 * head_width).swapaxes(0, 1)
    total = scatter(total, "lon").reshape(2, -1, 4 * head_width)
    pack_sum = total[:, :, : 3 * head_width].reshape(2, -1, 3, head_width)
    proj_sum = total[:, :, 3 * head_width :]
    return layer_out, unquads(input_grad.reshape(PARTS, -1, model_width)), pack_sum, proj_sum


def solution(mesh):
    in_specs = (
        P(None, "lat", "lon", None),
        P(None, "lat", "lon", None),
        P(None, None, None, "head"),
        P(None, None, "head"),
        P(None, None, "head"),
        P(None, None, "head"),
        P("lat", "lon"),
    )
    out_specs = (
        P(None, "lat", "lon", None),
        P(None, "lat", "lon", None),
        P(None, ("lat", "lon"), None, "head"),
        P(None, ("lat", "lon"), "head"),
    )
    return jax.shard_map(
        per_device, mesh=mesh, in_specs=in_specs, out_specs=out_specs, check_vma=False
    )
```

```python
from functools import partial

import jax
import jax.numpy as jnp
import numpy as np
from jax import lax
from jax.experimental import pallas as pl
from jax.experimental.pallas import tpu as pltpu
from jax.sharding import PartitionSpec as P

HD = 64
EPSILON = 1e-05
PARTS = 4
BF = jnp.bfloat16
F32 = jnp.float32


def norm_rows(values):
    average = jnp.mean(values, axis=-1, keepdims=True)
    centred = values - average
    spread = jnp.mean(centred * centred, axis=-1, keepdims=True)
    return centred * lax.rsqrt(spread + EPSILON)


def norm_pull(stream, cotangent):
    stream = stream.astype(F32)
    average = jnp.mean(stream, axis=-1, keepdims=True)
    centred = stream - average
    spread = jnp.mean(centred * centred, axis=-1, keepdims=True)
    inverse = lax.rsqrt(spread + EPSILON)
    unit = centred * inverse
    mean_c = jnp.mean(cotangent, axis=-1, keepdims=True)
    mean_u = jnp.mean(cotangent * unit, axis=-1, keepdims=True)
    return inverse * (cotangent - mean_c - unit * mean_u)


def dot(left, right, left_dim, right_dim):
    return lax.dot_general(
        left, right, (((left_dim,), (right_dim,)), ((), ())), preferred_element_type=F32
    )


def gelu_and_slope(pre):
    cdf = 0.5 * (1.0 + lax.erf(pre * 0.7071067811865476))
    density = jnp.exp(-0.5 * pre * pre) * 0.3989422804014327
    return pre * cdf, cdf + pre * density


def quads(grid):
    channels = grid.shape[-1]
    return (
        grid.reshape(-1, 2, 3, 2, 6, channels).transpose(1, 3, 0, 2, 4, 5).reshape(PARTS, -1, channels)
    )


def unquads(rows):
    channels = rows.shape[-1]
    return (
        rows.reshape(2, 2, -1, 3, 6, channels)
        .transpose(2, 0, 3, 1, 4, 5)
        .reshape(-1, 6, 12, channels)
    )


def joint(sizes, move):
    pairs = []
    for source in np.ndindex(*sizes):
        target = [t % s for t, s in zip(move(*source), sizes)]
        pairs.append((int(np.ravel_multi_index(source, sizes)), int(np.ravel_multi_index(target, sizes))))
    return pairs


def after(value, *others):
    return lax.optimization_barrier((value,) + others)[0]


def send_quads(pieces, sign):
    sizes = (lax.axis_size("lat"), lax.axis_size("lon"))
    out = [pieces[0]]
    for q in (3, 2, 1):
        perm = joint(sizes, lambda a, b: (a + sign * (q // 2), b + sign * (q % 2)))
        out.insert(1, lax.ppermute(pieces[q], ("lat", "lon"), perm))
    return out


def lat_parts():
    lats = lax.axis_size("lat")
    return 2, lats // 2


def fetch_heads(shard, gate=()):
    low, ring = lat_parts()
    sizes = (low * ring, lax.axis_size("head"))
    shard = after(shard, *gate)

    def odd(hops):
        def move(a, h):
            low_now, x = divmod(a, ring)
            return ((1 - low_now) * ring + x, h + (hops if low_now else -hops))

        return joint(sizes, move)

    def even(a, h):
        return (a, h + (1 if a // ring else -1))

    three = lax.ppermute(shard, ("lat", "head"), odd(2))
    two = lax.ppermute(shard, ("lat", "head"), joint(sizes, even))
    one = lax.ppermute(shard, ("lat", "head"), odd(1))
    return one, two, three


def swap_cores(piece):
    size = lax.axis_size("lon")
    return lax.ppermute(piece, "lon", [(i, i ^ 1) for i in range(size)])


def ring_x(own, long_way, gates=((), ())):
    low, ring = lat_parts()
    size = lax.axis_size("lat")

    def pairs(by):
        return [(i, i // ring * ring + (i + by) % ring) for i in range(size)]

    blocks = {0: own}
    for sign, gate in zip((long_way, -long_way), gates):
        if ring > 2 or sign == long_way:
            sent = after(own, *gate)
            blocks[sign % ring] = lax.ppermute(sent, "lat", pairs(sign))
    if ring > 2:
        blocks[2] = lax.ppermute(blocks[long_way % ring], "lat", pairs(long_way))
    return [blocks[s] for s in range(ring)]


def shard_kernel(ring, qkv_ref, proj_ref, up_ref, down_ref, *refs):
    out_ref, sem = refs
    rows, half = out_ref.shape[1:]
    side = lax.axis_index("lon") % 2
    start = pl.multiple_of(lax.axis_index("lat") % ring * rows, rows)
    width, hidden = proj_ref.shape[2], up_ref.shape[2]
    split = half - 4 * width

    def run(views):
        copies = []
        for layer in range(2):
            at = 0
            for view in views(layer):
                target = out_ref.at[layer, :, pl.ds(at, view.shape[1])]
                copies.append(pltpu.make_async_copy(view, target, sem.at[len(copies)]))
                at += view.shape[1]
        for copy in copies:
            copy.start()
        for copy in copies:
            copy.wait()

    @pl.when(side == 0)
    def _():
        run(
            lambda layer: [qkv_ref.at[layer, i, pl.ds(start, rows), :] for i in range(3)]
            + [proj_ref.at[layer, pl.ds(start, rows), :], up_ref.at[layer, pl.ds(start, rows), pl.ds(0, split)]]
        )

    @pl.when(side == 1)
    def _():
        run(
            lambda layer: [
                up_ref.at[layer, pl.ds(start, rows), pl.ds(split, hidden - split)],
                down_ref.at[layer, pl.ds(start, rows), :],
            ]
        )


def weight_shards(own):
    ring = lat_parts()[1]
    columns = 4 * own[1].shape[2] + 2 * own[2].shape[2]
    shard = jax.ShapeDtypeStruct((2, own[1].shape[1] // ring, columns // 2), BF)
    return pl.pallas_call(
        partial(shard_kernel, ring),
        out_shape=shard,
        in_specs=hbm_specs(4),
        out_specs=pl.BlockSpec(memory_space=pltpu.VMEM),
        scratch_shapes=[pltpu.SemaphoreType.DMA((10,))],
        compiler_params=pltpu.CompilerParams(vmem_limit_bytes=58 * 1024 * 1024),
    )(*own)


def pack_kernel(*refs):
    in_refs, out_refs, sem = refs[:-3], refs[-3:-1], refs[-1]
    copies = []
    for k, ref in enumerate(in_refs):
        for layer, out_ref in enumerate(out_refs):
            copies.append(pltpu.make_async_copy(ref.at[layer], out_ref.at[k], sem.at[len(copies)]))
    for copy in copies:
        copy.start()
    for copy in copies:
        copy.wait()


def pack_shards(fetched):
    block = jax.ShapeDtypeStruct((len(fetched),) + fetched[0].shape[1:], BF)
    return pl.pallas_call(
        pack_kernel,
        out_shape=[block] * 2,
        in_specs=any_specs(len(fetched)),
        out_specs=any_specs(2),
        scratch_shapes=[pltpu.SemaphoreType.DMA((2 * len(fetched),))],
        compiler_params=pltpu.CompilerParams(vmem_limit_bytes=4 * 1024 * 1024),
    )(*fetched)


def load_weights(layer, piece_refs, own_refs, w_ref, sem):
    ring = len(piece_refs) // 2
    rows, half = piece_refs[0].shape[1:]
    core = lax.axis_index("lon") % 2
    place = lax.axis_index("lat") % ring
    copies = []
    at = 0
    for ref in own_refs:
        views = [ref.at[layer, i] for i in range(3)] if len(ref.shape) == 4 else [ref.at[layer]]
        for view in views:
            copies.append((view, w_ref.at[0, :, pl.ds(at, view.shape[1])]))
            at += view.shape[1]
    for s in range(ring):
        start = pl.multiple_of((place - s + ring) % ring * rows, rows)
        for side, ref in ((core, piece_refs[s]), (1 - core, piece_refs[ring + s])):
            columns = pl.ds(pl.multiple_of(side * half, half), half)
            copies.append((ref, w_ref.at[pl.ds(1, PARTS - 1), pl.ds(start, rows), columns]))
    copies = [pltpu.make_async_copy(s, d, sem.at[i]) for i, (s, d) in enumerate(copies)]
    for copy in copies:
        copy.start()
    return copies


class Weights:
    def __init__(self, ref, ends):
        self.ref = ref
        self.ends = ends

    def get(self, k, which):
        return self.ref[k, :, self.ends[which] : self.ends[which + 1]]

    qkv = lambda self, k: self.get(k, 0)
    proj = lambda self, k: self.get(k, 1)
    up = lambda self, k: self.get(k, 2)
    down = lambda self, k: self.get(k, 3)


def head_parts(packed, a):
    width = packed.shape[1] // 3
    return tuple(packed[:, i * width + a * HD : i * width + (a + 1) * HD] for i in range(3))


def forward(x, weights, allowed, packed_ref, probs_ref, mixed_ref, slope_ref):
    normed = norm_rows(x).astype(BF)
    total = jnp.zeros(x.shape, F32)
    for k in range(PARTS):
        packed = dot(normed, weights.qkv(k), 1, 0).astype(BF)
        packed_ref[k] = packed
        count = packed.shape[1] // (3 * HD)
        outs = []
        for a in range(count):
            queries, keys, values = head_parts(packed, a)
            scores = dot(queries, keys, 1, 1) * HD**-0.5
            if allowed is not None:
                scores = jnp.where(allowed, scores, -1e30)
            exps = jnp.exp(scores - jnp.max(scores, axis=-1, keepdims=True))
            probs = exps / jnp.sum(exps, axis=-1, keepdims=True)
            probs_ref[k * count + a] = probs.astype(probs_ref.dtype)
            outs.append(dot(probs.astype(BF), values, 1, 0))
        mixed = jnp.concatenate(outs, axis=1).astype(BF)
        if k == 0:
            mixed_ref[...] = mixed
        total += dot(mixed, weights.proj(k), 1, 1)
    middle = (x + total).astype(BF)
    second = norm_rows(middle.astype(F32)).astype(BF)
    total = jnp.zeros(x.shape, F32)
    for k in range(PARTS):
        active, slope = gelu_and_slope(dot(second, weights.up(k), 1, 0))
        slope_ref[k] = slope.astype(slope_ref.dtype)
        total += dot(active.astype(BF), weights.down(k), 1, 1)
    return middle, (middle.astype(F32) + total).astype(BF)


def backward(x, middle, gradient, weights, factor, packed_ref, probs_ref, mixed_ref, slope_ref, sums_ref):
    middle = middle.astype(F32)
    total = jnp.zeros(x.shape, F32)
    for k in range(PARTS):
        d_pre = (slope_ref[k].astype(F32) * dot(gradient, weights.down(k), 1, 0)).astype(BF)
        total += dot(d_pre, weights.up(k), 1, 1)
    mid_grad = (gradient.astype(F32) + norm_pull(middle, total)).astype(BF)
    total = jnp.zeros(x.shape, F32)
    for k in range(PARTS):
        d_mixed = dot(mid_grad, weights.proj(k), 1, 0).astype(BF)
        packed = packed_ref[k]
        width = d_mixed.shape[1]
        count = width // HD
        parts = [[], [], []]
        for a in range(count):
            queries, keys, values = head_parts(packed, a)
            d_out = d_mixed[:, a * HD : (a + 1) * HD]
            probs = probs_ref[k * count + a].astype(F32)
            d_probs = dot(d_out, values, 1, 1)
            d_scores = probs * (d_probs - jnp.sum(d_probs * probs, axis=-1, keepdims=True))
            d_scores = (d_scores * HD**-0.5).astype(BF)
            parts[0].append(dot(d_scores, keys, 1, 0))
            parts[1].append(dot(d_scores, queries, 0, 0))
            parts[2].append(dot(probs.astype(BF), d_out, 0, 0))
        d_packed = jnp.concatenate(parts[0] + parts[1] + parts[2], axis=1).astype(BF)
        total += dot(d_packed, weights.qkv(k), 1, 1)
        if k == 0:
            normed = norm_rows(x).astype(BF)
            first = (dot(normed, d_packed, 0, 0) * factor).astype(BF)
            second = (dot(mid_grad, mixed_ref[...], 0, 0) * factor).astype(BF)
            if len(sums_ref.shape) == 2:
                sums_ref[:, : 3 * width] = first
                sums_ref[:, 3 * width :] = second
            else:
                lats, _, rows, _ = sums_ref.shape
                sums_ref[:, 0, :, : 3 * width] = first.reshape(lats, rows, 3 * width)
                sums_ref[:, 0, :, 3 * width :] = second.reshape(lats, rows, width)
    return (mid_grad.astype(F32) + norm_pull(x, total)).astype(BF)


def first_kernel(pieces, ends, *refs):
    x_ref, refs = refs[0], refs[1:]
    piece_refs, own_refs, refs = refs[:pieces], refs[pieces : pieces + 4], refs[pieces + 4 :]
    out_refs, (middle_ref, *saved), (w_ref, sem) = refs[:PARTS], refs[PARTS:-2], refs[-2:]
    copies = load_weights(0, piece_refs, own_refs, w_ref, sem)
    for copy in copies:
        copy.wait()
    middle, out = forward(x_ref[...].astype(F32), Weights(w_ref, ends), None, *saved)
    middle_ref[...] = middle
    rows = out.shape[0] // PARTS
    for q in range(PARTS):
        out_refs[q][...] = out[q * rows : (q + 1) * rows]


def second_kernel(pieces, ends, factor, *refs):
    x_refs, grad_refs, refs = refs[:PARTS], refs[PARTS : 2 * PARTS], refs[2 * PARTS :]
    mask_ref, *refs = refs
    piece_refs, own_refs, refs = refs[:pieces], refs[pieces : pieces + 4], refs[pieces + 4 :]
    out_refs, (sums_ref, w_ref, *saved), sem = refs[:PARTS], refs[PARTS:-1], refs[-1]
    copies = load_weights(1, piece_refs, own_refs, w_ref, sem)
    x = jnp.concatenate([ref[...].astype(F32) for ref in x_refs], axis=0)
    allowed = mask_ref[...] > 0
    for copy in copies:
        copy.wait()
    weights = Weights(w_ref, ends)
    middle, out = forward(x, weights, allowed, *saved)
    rows = out.shape[0] // PARTS
    for q in range(PARTS):
        out_refs[q][0] = out[q * rows : (q + 1) * rows]
    gradient = jnp.concatenate([ref[...].astype(F32) for ref in grad_refs], axis=0).astype(BF)
    result = backward(x, middle, gradient, weights, factor, *saved, sums_ref)
    for q in range(PARTS):
        out_refs[q][1] = result[q * rows : (q + 1) * rows]


def third_kernel(pieces, ends, factor, *refs):
    grad_refs, (late_ref, x_ref), refs = refs[:PARTS], refs[PARTS : PARTS + 2], refs[PARTS + 2 :]
    (middle_ref, *saved), refs = refs[:5], refs[5:]
    piece_refs, own_refs, refs = refs[:pieces], refs[pieces : pieces + 4], refs[pieces + 4 :]
    result_ref, sums_ref, w_ref, sem = refs
    copies = load_weights(0, piece_refs, own_refs, w_ref, sem)
    gradient = jnp.concatenate([ref[1].astype(F32) for ref in grad_refs], axis=0).astype(BF)
    lats, _, rows, columns = sums_ref.shape
    sums_ref[:, 1] = late_ref[...].reshape(lats, rows, columns)
    for copy in copies:
        copy.wait()
    weights = Weights(w_ref, ends)
    result_ref[...] = backward(
        x_ref[...].astype(F32), middle_ref[...], gradient, weights, factor, *saved, sums_ref
    )


def vmem_specs(count):
    return [pl.BlockSpec(memory_space=pltpu.VMEM)] * count


def any_specs(count):
    return [pl.BlockSpec(memory_space=pl.ANY)] * count


def hbm_specs(count):
    return [pl.BlockSpec(memory_space=pltpu.HBM)] * count


PARAMS = pltpu.CompilerParams(vmem_limit_bytes=36 * 1024 * 1024)


def cost(flops):
    return pl.CostEstimate(flops=flops, bytes_accessed=8_000_000, transcendentals=600_000)


def scatter(parts, axis):
    size = lax.axis_size(axis)
    parts = parts.reshape(size, -1, parts.shape[-1])
    return jnp.sum(lax.all_to_all(parts, axis, 0, 0).astype(F32), axis=0)


def per_device(inputs, cotangent, qkv_weight, proj_weight, up_weight, down_weight, shift_labels):
    level_count, lat_rows, lon_cols, model_width = inputs.shape
    head_width = qkv_weight.shape[-1]
    tokens = level_count * lat_rows * lon_cols
    quarter = tokens // PARTS
    factor = float(tokens * lax.axis_size("lat") * lax.axis_size("lon")) ** -0.5

    own = (qkv_weight.swapaxes(1, 2), proj_weight, up_weight, down_weight)
    ends = [0, 3 * head_width, 4 * head_width]
    ends = ends + [ends[-1] + up_weight.shape[2], ends[-1] + 2 * up_weight.shape[2]]
    fetched = fetch_heads(weight_shards(own))
    ending = send_quads(list(after(quads(cotangent), fetched[0])), 1)
    edge = ((jnp.arange(lat_rows) < 3) & (lax.axis_index("lat") == 0)).astype(jnp.int32)
    region = jnp.broadcast_to((shift_labels * 2 + edge[:, None])[None, :, :, None], (level_count, 6, 12, 1))
    labels = quads(region)[::-1].reshape(-1)
    mask = (labels[:, None] == labels[None, :]).astype(F32)
    start = quads(inputs).reshape(tokens, model_width)
    *fetched, start, mask, e0, e1, e2, e3 = lax.optimization_barrier((*fetched, start, mask, *ending))
    ending = (e0, e1, e2, e3)
    early_block, late_block = pack_shards(fetched)
    early_ring = ring_x(early_block, 1)
    late_ring = ring_x(late_block, -1, (early_ring[1::2], early_ring[2:3]))
    early_all = early_ring + [swap_cores(piece) for piece in early_ring]
    late_swaps = {s: swap_cores(late_ring[s]) for s in (0, len(late_ring) - 1)}
    start = after(start, *late_swaps.values())

    width = head_width // HD * PARTS
    stream = jax.ShapeDtypeStruct((tokens, model_width), BF)
    piece = jax.ShapeDtypeStruct((quarter, model_width), BF)
    pair = jax.ShapeDtypeStruct((2, quarter, model_width), BF)
    sums = jax.ShapeDtypeStruct((model_width, 4 * head_width), BF)
    weight_space = pltpu.VMEM((PARTS, model_width, ends[-1]), BF)
    saved = [
        jax.ShapeDtypeStruct((PARTS, tokens, 3 * head_width), BF),
        jax.ShapeDtypeStruct((width, tokens, tokens), F32),
        jax.ShapeDtypeStruct((tokens, head_width), BF),
        jax.ShapeDtypeStruct((PARTS, tokens, up_weight.shape[2]), F32),
    ]
    held = [jax.ShapeDtypeStruct(s.shape, BF) for s in saved]
    pieces = len(early_all)
    semaphores = pltpu.SemaphoreType.DMA((pieces + 6,))

    *quarters, middle, packed, probs, mixed, slope = pl.pallas_call(
        partial(first_kernel, pieces, ends),
        out_shape=[piece] * PARTS + [stream] + held,
        in_specs=vmem_specs(1) + any_specs(pieces) + hbm_specs(4),
        out_specs=vmem_specs(PARTS + 5),
        scratch_shapes=[weight_space, semaphores],
        compiler_params=PARAMS,
        cost_estimate=cost(1_800_000_000),
    )(start, *early_all, *own)
    quarters = send_quads(quarters, 1)
    for s, piece in enumerate(late_ring):
        if s not in late_swaps:
            late_swaps[s] = swap_cores(after(piece, *quarters[1:]))
    late_all = late_ring + [late_swaps[s] for s in range(len(late_ring))]
    *pairs, late_sum = pl.pallas_call(
        partial(second_kernel, pieces, ends, factor),
        out_shape=[pair] * PARTS + [sums],
        in_specs=vmem_specs(2 * PARTS + 1) + any_specs(pieces) + hbm_specs(4),
        out_specs=vmem_specs(PARTS + 1),
        scratch_shapes=[weight_space] + [pltpu.VMEM(s.shape, s.dtype) for s in saved] + [semaphores],
        compiler_params=PARAMS,
        cost_estimate=cost(3_800_000_000),
    )(*quarters, *ending, mask, *late_all, *own)
    pairs = send_quads(pairs, -1)
    lats, lons = lax.axis_size("lat"), lax.axis_size("lon")
    both = jax.ShapeDtypeStruct((lats, 2, model_width // lats, 4 * head_width), BF)
    input_grad, total = pl.pallas_call(
        partial(third_kernel, pieces, ends, factor),
        out_shape=[stream, both],
        in_specs=vmem_specs(PARTS + 7) + any_specs(pieces) + hbm_specs(4),
        out_specs=vmem_specs(2),
        scratch_shapes=[weight_space, semaphores],
        compiler_params=PARAMS,
        cost_estimate=cost(2_000_000_000),
    )(*pairs, late_sum, start, middle, packed, probs, mixed, slope, *early_all, *own)

    layer_out = unquads(jnp.stack([p[0] for p in pairs]))
    total = scatter(total, "lat").astype(BF).reshape(2, lons, -1, 4 * head_width).swapaxes(0, 1)
    total = scatter(total, "lon").reshape(2, -1, 4 * head_width)
    pack_sum = total[:, :, : 3 * head_width].reshape(2, -1, 3, head_width)
    proj_sum = total[:, :, 3 * head_width :]
    return layer_out, unquads(input_grad.reshape(PARTS, -1, model_width)), pack_sum, proj_sum


def solution(mesh):
    in_specs = (
        P(None, "lat", "lon", None),
        P(None, "lat", "lon", None),
        P(None, None, None, "head"),
        P(None, None, "head"),
        P(None, None, "head"),
        P(None, None, "head"),
        P("lat", "lon"),
    )
    out_specs = (
        P(None, "lat", "lon", None),
        P(None, "lat", "lon", None),
        P(None, ("lat", "lon"), None, "head"),
        P(None, ("lat", "lon"), "head"),
    )
    return jax.shard_map(
        per_device, mesh=mesh, in_specs=in_specs, out_specs=out_specs, check_vma=False
    )
```

```python
from functools import partial

import jax
import jax.numpy as jnp
import numpy as np
from jax import lax
from jax.experimental import pallas as pl
from jax.experimental.pallas import tpu as pltpu
from jax.sharding import PartitionSpec as P

HD = 64
EPSILON = 1e-05
PARTS = 4
BF = jnp.bfloat16
F32 = jnp.float32


def norm_rows(values):
    average = jnp.mean(values, axis=-1, keepdims=True)
    centred = values - average
    spread = jnp.mean(centred * centred, axis=-1, keepdims=True)
    return centred * lax.rsqrt(spread + EPSILON)


def norm_pull(stream, cotangent):
    stream = stream.astype(F32)
    average = jnp.mean(stream, axis=-1, keepdims=True)
    centred = stream - average
    spread = jnp.mean(centred * centred, axis=-1, keepdims=True)
    inverse = lax.rsqrt(spread + EPSILON)
    unit = centred * inverse
    mean_c = jnp.mean(cotangent, axis=-1, keepdims=True)
    mean_u = jnp.mean(cotangent * unit, axis=-1, keepdims=True)
    return inverse * (cotangent - mean_c - unit * mean_u)


def dot(left, right, left_dim, right_dim):
    return lax.dot_general(
        left, right, (((left_dim,), (right_dim,)), ((), ())), preferred_element_type=F32
    )


def gelu_and_slope(pre):
    cdf = 0.5 * (1.0 + lax.erf(pre * 0.7071067811865476))
    density = jnp.exp(-0.5 * pre * pre) * 0.3989422804014327
    return pre * cdf, cdf + pre * density


def quads(grid):
    channels = grid.shape[-1]
    return (
        grid.reshape(-1, 2, 3, 2, 6, channels).transpose(1, 3, 0, 2, 4, 5).reshape(PARTS, -1, channels)
    )


def unquads(rows):
    channels = rows.shape[-1]
    return (
        rows.reshape(2, 2, -1, 3, 6, channels)
        .transpose(2, 0, 3, 1, 4, 5)
        .reshape(-1, 6, 12, channels)
    )


def joint(sizes, move):
    pairs = []
    for source in np.ndindex(*sizes):
        target = [t % s for t, s in zip(move(*source), sizes)]
        pairs.append((int(np.ravel_multi_index(source, sizes)), int(np.ravel_multi_index(target, sizes))))
    return pairs


def after(value, *others):
    return lax.optimization_barrier((value,) + others)[0]


def send_quads(pieces, sign):
    sizes = (lax.axis_size("lat"), lax.axis_size("lon"))
    out = [pieces[0]]
    for q in (3, 2, 1):
        perm = joint(sizes, lambda a, b: (a + sign * (q // 2), b + sign * (q % 2)))
        out.insert(1, lax.ppermute(pieces[q], ("lat", "lon"), perm))
    return out


def lat_parts():
    lats = lax.axis_size("lat")
    return 2, lats // 2


def fetch_heads(shard, gate=()):
    low, ring = lat_parts()
    sizes = (low * ring, lax.axis_size("head"))
    shard = after(shard, *gate)

    def odd(hops):
        def move(a, h):
            low_now, x = divmod(a, ring)
            return ((1 - low_now) * ring + x, h + (hops if low_now else -hops))

        return joint(sizes, move)

    def even(a, h):
        return (a, h + (1 if a // ring else -1))

    three = lax.ppermute(shard, ("lat", "head"), odd(2))
    two = lax.ppermute(shard, ("lat", "head"), joint(sizes, even))
    one = lax.ppermute(shard, ("lat", "head"), odd(1))
    return one, two, three


def swap_cores(piece):
    size = lax.axis_size("lon")
    return lax.ppermute(piece, "lon", [(i, i ^ 1) for i in range(size)])


def along_x(block, by):
    ring, size = lat_parts()[1], lax.axis_size("lat")
    return lax.ppermute(block, "lat", [(i, i // ring * ring + (i + by) % ring) for i in range(size)])


def ring_near(own):
    ring = lat_parts()[1]
    blocks = {0: own, 1 % ring: along_x(own, 1)}
    if ring > 2:
        blocks[ring - 1] = along_x(own, -1)
    return blocks


def ring_far(blocks, by, *gate):
    ring = lat_parts()[1]
    if ring > 2:
        blocks[2] = along_x(after(blocks[by % ring], *gate), by)
    return [blocks[s] for s in range(ring)]


def shard_kernel(ring, qkv_ref, proj_ref, up_ref, down_ref, *refs):
    out_refs, sem = refs[:-1], refs[-1]
    rows, half = out_refs[0].shape
    side = lax.axis_index("lon") % 2
    start = pl.multiple_of(lax.axis_index("lat") % ring * rows, rows)
    width, hidden = proj_ref.shape[2], up_ref.shape[2]
    split = half - 4 * width

    def run(views):
        copies = []
        for layer, out_ref in enumerate(out_refs):
            at = 0
            for view in views(layer):
                target = out_ref.at[:, pl.ds(at, view.shape[1])]
                copies.append(pltpu.make_async_copy(view, target, sem.at[len(copies)]))
                at += view.shape[1]
        for copy in copies:
            copy.start()
        for copy in copies:
            copy.wait()

    @pl.when(side == 0)
    def _():
        run(
            lambda layer: [qkv_ref.at[layer, i, pl.ds(start, rows), :] for i in range(3)]
            + [proj_ref.at[layer, pl.ds(start, rows), :], up_ref.at[layer, pl.ds(start, rows), pl.ds(0, split)]]
        )

    @pl.when(side == 1)
    def _():
        run(
            lambda layer: [
                up_ref.at[layer, pl.ds(start, rows), pl.ds(split, hidden - split)],
                down_ref.at[layer, pl.ds(start, rows), :],
            ]
        )


def weight_shards(own):
    ring = lat_parts()[1]
    columns = 4 * own[1].shape[2] + 2 * own[2].shape[2]
    shard = jax.ShapeDtypeStruct((own[1].shape[1] // ring, columns // 2), BF)
    return pl.pallas_call(
        partial(shard_kernel, ring),
        out_shape=[shard] * 2,
        in_specs=hbm_specs(4),
        out_specs=vmem_specs(2),
        scratch_shapes=[pltpu.SemaphoreType.DMA((10,))],
        compiler_params=pltpu.CompilerParams(vmem_limit_bytes=58 * 1024 * 1024),
    )(*own)


def pack_kernel(*refs):
    in_refs, out_ref, sem = refs[:-2], refs[-2], refs[-1]
    copies = [pltpu.make_async_copy(ref, out_ref.at[k], sem.at[k]) for k, ref in enumerate(in_refs)]
    for copy in copies:
        copy.start()
    for copy in copies:
        copy.wait()


def pack_shards(fetched):
    return pl.pallas_call(
        pack_kernel,
        out_shape=jax.ShapeDtypeStruct((len(fetched),) + fetched[0].shape, BF),
        in_specs=any_specs(len(fetched)),
        out_specs=pl.BlockSpec(memory_space=pl.ANY),
        scratch_shapes=[pltpu.SemaphoreType.DMA((len(fetched),))],
        compiler_params=pltpu.CompilerParams(vmem_limit_bytes=4 * 1024 * 1024),
    )(*fetched)


def load_weights(layer, piece_refs, own_refs, w_ref, sem):
    ring = len(piece_refs) // 2
    rows, half = piece_refs[0].shape[1:]
    core = lax.axis_index("lon") % 2
    place = lax.axis_index("lat") % ring
    copies = []
    at = 0
    for ref in own_refs:
        views = [ref.at[layer, i] for i in range(3)] if len(ref.shape) == 4 else [ref.at[layer]]
        for view in views:
            copies.append((view, w_ref.at[0, :, pl.ds(at, view.shape[1])]))
            at += view.shape[1]
    for s in range(ring):
        start = pl.multiple_of((place - s + ring) % ring * rows, rows)
        for side, ref in ((core, piece_refs[s]), (1 - core, piece_refs[ring + s])):
            columns = pl.ds(pl.multiple_of(side * half, half), half)
            copies.append((ref, w_ref.at[pl.ds(1, PARTS - 1), pl.ds(start, rows), columns]))
    copies = [pltpu.make_async_copy(s, d, sem.at[i]) for i, (s, d) in enumerate(copies)]
    for copy in copies:
        copy.start()
    return copies


class Weights:
    def __init__(self, ref, ends):
        self.ref = ref
        self.ends = ends

    def get(self, k, which):
        return self.ref[k, :, self.ends[which] : self.ends[which + 1]]

    qkv = lambda self, k: self.get(k, 0)
    proj = lambda self, k: self.get(k, 1)
    up = lambda self, k: self.get(k, 2)
    down = lambda self, k: self.get(k, 3)


def head_parts(packed, a):
    width = packed.shape[1] // 3
    return tuple(packed[:, i * width + a * HD : i * width + (a + 1) * HD] for i in range(3))


def forward(x, weights, allowed, packed_ref, probs_ref, mixed_ref, slope_ref):
    normed = norm_rows(x).astype(BF)
    total = jnp.zeros(x.shape, F32)
    for k in range(PARTS):
        packed = dot(normed, weights.qkv(k), 1, 0).astype(BF)
        packed_ref[k] = packed
        count = packed.shape[1] // (3 * HD)
        outs = []
        for a in range(count):
            queries, keys, values = head_parts(packed, a)
            scores = dot(queries, keys, 1, 1) * HD**-0.5
            if allowed is not None:
                scores = jnp.where(allowed, scores, -1e30)
            exps = jnp.exp(scores - jnp.max(scores, axis=-1, keepdims=True))
            probs = exps / jnp.sum(exps, axis=-1, keepdims=True)
            probs_ref[k * count + a] = probs.astype(probs_ref.dtype)
            outs.append(dot(probs.astype(BF), values, 1, 0))
        mixed = jnp.concatenate(outs, axis=1).astype(BF)
        if k == 0:
            mixed_ref[...] = mixed
        total += dot(mixed, weights.proj(k), 1, 1)
    middle = (x + total).astype(BF)
    second = norm_rows(middle.astype(F32)).astype(BF)
    total = jnp.zeros(x.shape, F32)
    for k in range(PARTS):
        active, slope = gelu_and_slope(dot(second, weights.up(k), 1, 0))
        slope_ref[k] = slope.astype(slope_ref.dtype)
        total += dot(active.astype(BF), weights.down(k), 1, 1)
    return middle, (middle.astype(F32) + total).astype(BF)


def backward(x, middle, gradient, weights, factor, packed_ref, probs_ref, mixed_ref, slope_ref, sums_ref):
    middle = middle.astype(F32)
    total = jnp.zeros(x.shape, F32)
    for k in range(PARTS):
        d_pre = (slope_ref[k].astype(F32) * dot(gradient, weights.down(k), 1, 0)).astype(BF)
        total += dot(d_pre, weights.up(k), 1, 1)
    mid_grad = (gradient.astype(F32) + norm_pull(middle, total)).astype(BF)
    total = jnp.zeros(x.shape, F32)
    for k in range(PARTS):
        d_mixed = dot(mid_grad, weights.proj(k), 1, 0).astype(BF)
        packed = packed_ref[k]
        width = d_mixed.shape[1]
        count = width // HD
        parts = [[], [], []]
        for a in range(count):
            queries, keys, values = head_parts(packed, a)
            d_out = d_mixed[:, a * HD : (a + 1) * HD]
            probs = probs_ref[k * count + a].astype(F32)
            d_probs = dot(d_out, values, 1, 1)
            d_scores = probs * (d_probs - jnp.sum(d_probs * probs, axis=-1, keepdims=True))
            d_scores = (d_scores * HD**-0.5).astype(BF)
            parts[0].append(dot(d_scores, keys, 1, 0))
            parts[1].append(dot(d_scores, queries, 0, 0))
            parts[2].append(dot(probs.astype(BF), d_out, 0, 0))
        d_packed = jnp.concatenate(parts[0] + parts[1] + parts[2], axis=1).astype(BF)
        total += dot(d_packed, weights.qkv(k), 1, 1)
        if k == 0:
            normed = norm_rows(x).astype(BF)
            first = (dot(normed, d_packed, 0, 0) * factor).astype(BF)
            second = (dot(mid_grad, mixed_ref[...], 0, 0) * factor).astype(BF)
            if len(sums_ref.shape) == 2:
                sums_ref[:, : 3 * width] = first
                sums_ref[:, 3 * width :] = second
            else:
                lats, _, rows, _ = sums_ref.shape
                sums_ref[:, 0, :, : 3 * width] = first.reshape(lats, rows, 3 * width)
                sums_ref[:, 0, :, 3 * width :] = second.reshape(lats, rows, width)
    return (mid_grad.astype(F32) + norm_pull(x, total)).astype(BF)


def first_kernel(pieces, ends, *refs):
    x_ref, refs = refs[0], refs[1:]
    piece_refs, own_refs, refs = refs[:pieces], refs[pieces : pieces + 4], refs[pieces + 4 :]
    out_refs, (middle_ref, *saved), (w_ref, sem) = refs[:PARTS], refs[PARTS:-2], refs[-2:]
    copies = load_weights(0, piece_refs, own_refs, w_ref, sem)
    for copy in copies:
        copy.wait()
    middle, out = forward(x_ref[...].astype(F32), Weights(w_ref, ends), None, *saved)
    middle_ref[...] = middle
    rows = out.shape[0] // PARTS
    for q in range(PARTS):
        out_refs[q][...] = out[q * rows : (q + 1) * rows]


def second_kernel(pieces, ends, factor, *refs):
    x_refs, grad_refs, refs = refs[:PARTS], refs[PARTS : 2 * PARTS], refs[2 * PARTS :]
    mask_ref, *refs = refs
    piece_refs, own_refs, refs = refs[:pieces], refs[pieces : pieces + 4], refs[pieces + 4 :]
    out_refs, (sums_ref, w_ref, *saved), sem = refs[:PARTS], refs[PARTS:-1], refs[-1]
    copies = load_weights(1, piece_refs, own_refs, w_ref, sem)
    x = jnp.concatenate([ref[...].astype(F32) for ref in x_refs], axis=0)
    allowed = mask_ref[...] > 0
    for copy in copies:
        copy.wait()
    weights = Weights(w_ref, ends)
    middle, out = forward(x, weights, allowed, *saved)
    rows = out.shape[0] // PARTS
    for q in range(PARTS):
        out_refs[q][0] = out[q * rows : (q + 1) * rows]
    gradient = jnp.concatenate([ref[...].astype(F32) for ref in grad_refs], axis=0).astype(BF)
    result = backward(x, middle, gradient, weights, factor, *saved, sums_ref)
    for q in range(PARTS):
        out_refs[q][1] = result[q * rows : (q + 1) * rows]


def third_kernel(pieces, ends, factor, *refs):
    grad_refs, (late_ref, x_ref), refs = refs[:PARTS], refs[PARTS : PARTS + 2], refs[PARTS + 2 :]
    (middle_ref, *saved), refs = refs[:5], refs[5:]
    piece_refs, own_refs, refs = refs[:pieces], refs[pieces : pieces + 4], refs[pieces + 4 :]
    result_ref, sums_ref, w_ref, sem = refs
    copies = load_weights(0, piece_refs, own_refs, w_ref, sem)
    gradient = jnp.concatenate([ref[1].astype(F32) for ref in grad_refs], axis=0).astype(BF)
    lats, _, rows, columns = sums_ref.shape
    sums_ref[:, 1] = late_ref[...].reshape(lats, rows, columns)
    for copy in copies:
        copy.wait()
    weights = Weights(w_ref, ends)
    result_ref[...] = backward(
        x_ref[...].astype(F32), middle_ref[...], gradient, weights, factor, *saved, sums_ref
    )


def vmem_specs(count):
    return [pl.BlockSpec(memory_space=pltpu.VMEM)] * count


def any_specs(count):
    return [pl.BlockSpec(memory_space=pl.ANY)] * count


def hbm_specs(count):
    return [pl.BlockSpec(memory_space=pltpu.HBM)] * count


PARAMS = pltpu.CompilerParams(vmem_limit_bytes=36 * 1024 * 1024)


def cost(flops):
    return pl.CostEstimate(flops=flops, bytes_accessed=8_000_000, transcendentals=600_000)


def scatter(parts, axis):
    size = lax.axis_size(axis)
    parts = parts.reshape(size, -1, parts.shape[-1])
    return jnp.sum(lax.all_to_all(parts, axis, 0, 0).astype(F32), axis=0)


def per_device(inputs, cotangent, qkv_weight, proj_weight, up_weight, down_weight, shift_labels):
    level_count, lat_rows, lon_cols, model_width = inputs.shape
    head_width = qkv_weight.shape[-1]
    tokens = level_count * lat_rows * lon_cols
    quarter = tokens // PARTS
    factor = float(tokens * lax.axis_size("lat") * lax.axis_size("lon")) ** -0.5

    own = (qkv_weight.swapaxes(1, 2), proj_weight, up_weight, down_weight)
    ends = [0, 3 * head_width, 4 * head_width]
    ends = ends + [ends[-1] + up_weight.shape[2], ends[-1] + 2 * up_weight.shape[2]]
    shards = weight_shards(own)
    early = fetch_heads(shards[0])
    ending = send_quads(list(after(quads(cotangent), shards[0])), 1)
    edge = ((jnp.arange(lat_rows) < 3) & (lax.axis_index("lat") == 0)).astype(jnp.int32)
    region = jnp.broadcast_to((shift_labels * 2 + edge[:, None])[None, :, :, None], (level_count, 6, 12, 1))
    labels = quads(region)[::-1].reshape(-1)
    mask = (labels[:, None] == labels[None, :]).astype(F32)
    start = quads(inputs).reshape(tokens, model_width)
    *early, start, mask, e0, e1, e2, e3 = lax.optimization_barrier((*early, start, mask, *ending))
    ending = (e0, e1, e2, e3)
    early_block = pack_shards(early)
    early_ring = ring_far(ring_near(early_block), 1)
    early_swaps = [swap_cores(early_block)]
    late = fetch_heads(shards[1], early_swaps)
    late = lax.optimization_barrier((*late, *early_ring[1:]))[:3]
    late_near = ring_near(pack_shards(late))
    early_all = early_ring + early_swaps + [swap_cores(piece) for piece in early_ring[1:]]

    width = head_width // HD * PARTS
    stream = jax.ShapeDtypeStruct((tokens, model_width), BF)
    piece = jax.ShapeDtypeStruct((quarter, model_width), BF)
    pair = jax.ShapeDtypeStruct((2, quarter, model_width), BF)
    sums = jax.ShapeDtypeStruct((model_width, 4 * head_width), BF)
    weight_space = pltpu.VMEM((PARTS, model_width, ends[-1]), BF)
    saved = [
        jax.ShapeDtypeStruct((PARTS, tokens, 3 * head_width), BF),
        jax.ShapeDtypeStruct((width, tokens, tokens), F32),
        jax.ShapeDtypeStruct((tokens, head_width), BF),
        jax.ShapeDtypeStruct((PARTS, tokens, up_weight.shape[2]), F32),
    ]
    held = [jax.ShapeDtypeStruct(s.shape, BF) for s in saved]
    pieces = len(early_all)
    semaphores = pltpu.SemaphoreType.DMA((pieces + 6,))

    *quarters, middle, packed, probs, mixed, slope = pl.pallas_call(
        partial(first_kernel, pieces, ends),
        out_shape=[piece] * PARTS + [stream] + held,
        in_specs=vmem_specs(1) + any_specs(pieces) + hbm_specs(4),
        out_specs=vmem_specs(PARTS + 5),
        scratch_shapes=[weight_space, semaphores],
        compiler_params=PARAMS,
        cost_estimate=cost(1_800_000_000),
    )(start, *early_all, *own)
    late_ring = ring_far(late_near, -1, quarters[0])
    quarters = send_quads(quarters, 1)
    late_swaps = [swap_cores(piece if s == 2 else after(piece, *quarters[1:])) for s, piece in enumerate(late_ring)]
    late_all = late_ring + late_swaps
    *pairs, late_sum = pl.pallas_call(
        partial(second_kernel, pieces, ends, factor),
        out_shape=[pair] * PARTS + [sums],
        in_specs=vmem_specs(2 * PARTS + 1) + any_specs(pieces) + hbm_specs(4),
        out_specs=vmem_specs(PARTS + 1),
        scratch_shapes=[weight_space] + [pltpu.VMEM(s.shape, s.dtype) for s in saved] + [semaphores],
        compiler_params=PARAMS,
        cost_estimate=cost(3_800_000_000),
    )(*quarters, *ending, mask, *late_all, *own)
    pairs = send_quads(pairs, -1)
    lats, lons = lax.axis_size("lat"), lax.axis_size("lon")
    both = jax.ShapeDtypeStruct((lats, 2, model_width // lats, 4 * head_width), BF)
    input_grad, total = pl.pallas_call(
        partial(third_kernel, pieces, ends, factor),
        out_shape=[stream, both],
        in_specs=vmem_specs(PARTS + 7) + any_specs(pieces) + hbm_specs(4),
        out_specs=vmem_specs(2),
        scratch_shapes=[weight_space, semaphores],
        compiler_params=PARAMS,
        cost_estimate=cost(2_000_000_000),
    )(*pairs, late_sum, start, middle, packed, probs, mixed, slope, *early_all, *own)

    layer_out = unquads(jnp.stack([p[0] for p in pairs]))
    total = scatter(total, "lat").astype(BF).reshape(2, lons, -1, 4 * head_width).swapaxes(0, 1)
    total = scatter(total, "lon").reshape(2, -1, 4 * head_width)
    pack_sum = total[:, :, : 3 * head_width].reshape(2, -1, 3, head_width)
    proj_sum = total[:, :, 3 * head_width :]
    return layer_out, unquads(input_grad.reshape(PARTS, -1, model_width)), pack_sum, proj_sum


def solution(mesh):
    in_specs = (
        P(None, "lat", "lon", None),
        P(None, "lat", "lon", None),
        P(None, None, None, "head"),
        P(None, None, "head"),
        P(None, None, "head"),
        P(None, None, "head"),
        P("lat", "lon"),
    )
    out_specs = (
        P(None, "lat", "lon", None),
        P(None, "lat", "lon", None),
        P(None, ("lat", "lon"), None, "head"),
        P(None, ("lat", "lon"), "head"),
    )
    return jax.shard_map(
        per_device, mesh=mesh, in_specs=in_specs, out_specs=out_specs, check_vma=False
    )
```

```python
from functools import partial

import jax
import jax.numpy as jnp
import numpy as np
from jax import lax
from jax.experimental import pallas as pl
from jax.experimental.pallas import tpu as pltpu
from jax.sharding import PartitionSpec as P

HD = 64
EPSILON = 1e-05
PARTS = 4
BF = jnp.bfloat16
F32 = jnp.float32


def norm_rows(values):
    average = jnp.mean(values, axis=-1, keepdims=True)
    centred = values - average
    spread = jnp.mean(centred * centred, axis=-1, keepdims=True)
    return centred * lax.rsqrt(spread + EPSILON)


def norm_pull(stream, cotangent):
    stream = stream.astype(F32)
    average = jnp.mean(stream, axis=-1, keepdims=True)
    centred = stream - average
    spread = jnp.mean(centred * centred, axis=-1, keepdims=True)
    inverse = lax.rsqrt(spread + EPSILON)
    unit = centred * inverse
    mean_c = jnp.mean(cotangent, axis=-1, keepdims=True)
    mean_u = jnp.mean(cotangent * unit, axis=-1, keepdims=True)
    return inverse * (cotangent - mean_c - unit * mean_u)


def dot(left, right, left_dim, right_dim):
    return lax.dot_general(
        left, right, (((left_dim,), (right_dim,)), ((), ())), preferred_element_type=F32
    )


def gelu_and_slope(pre):
    cdf = 0.5 * (1.0 + lax.erf(pre * 0.7071067811865476))
    density = jnp.exp(-0.5 * pre * pre) * 0.3989422804014327
    return pre * cdf, cdf + pre * density


def quads(grid):
    channels = grid.shape[-1]
    return (
        grid.reshape(-1, 2, 3, 2, 6, channels).transpose(1, 3, 0, 2, 4, 5).reshape(PARTS, -1, channels)
    )


def unquads(rows):
    channels = rows.shape[-1]
    return (
        rows.reshape(2, 2, -1, 3, 6, channels)
        .transpose(2, 0, 3, 1, 4, 5)
        .reshape(-1, 6, 12, channels)
    )


def joint(sizes, move):
    pairs = []
    for source in np.ndindex(*sizes):
        target = [t % s for t, s in zip(move(*source), sizes)]
        pairs.append((int(np.ravel_multi_index(source, sizes)), int(np.ravel_multi_index(target, sizes))))
    return pairs


def after(value, *others):
    return lax.optimization_barrier((value,) + others)[0]


def send_quads(pieces, sign):
    sizes = (lax.axis_size("lat"), lax.axis_size("lon"))
    out = [pieces[0]]
    for q in (3, 2, 1):
        perm = joint(sizes, lambda a, b: (a + sign * (q // 2), b + sign * (q % 2)))
        out.insert(1, lax.ppermute(pieces[q], ("lat", "lon"), perm))
    return out


def lat_parts():
    lats = lax.axis_size("lat")
    return 2, lats // 2


def fetch_heads(shard, gate=()):
    low, ring = lat_parts()
    sizes = (low * ring, lax.axis_size("head"))
    shard = after(shard, *gate)

    def odd(hops):
        def move(a, h):
            low_now, x = divmod(a, ring)
            return ((1 - low_now) * ring + x, h + (hops if low_now else -hops))

        return joint(sizes, move)

    def even(a, h):
        return (a, h + (1 if a // ring else -1))

    one = lax.ppermute(shard, ("lat", "head"), odd(1))
    two = lax.ppermute(shard, ("lat", "head"), joint(sizes, even))
    three = lax.ppermute(shard, ("lat", "head"), odd(2))
    return one, two, three


def swap_cores(piece):
    size = lax.axis_size("lon")
    return lax.ppermute(piece, "lon", [(i, i ^ 1) for i in range(size)])


def along_x(block, by):
    ring, size = lat_parts()[1], lax.axis_size("lat")
    return lax.ppermute(block, "lat", [(i, i // ring * ring + (i + by) % ring) for i in range(size)])


def ring_near(own, ahead=(), behind=()):
    ring = lat_parts()[1]
    blocks = {0: own, 1 % ring: along_x(after(own, *ahead), 1)}
    if ring > 2:
        blocks[ring - 1] = along_x(after(own, *behind), -1)
    return blocks


def ring_far(blocks, by, *gate):
    ring = lat_parts()[1]
    if ring > 2:
        blocks[2] = along_x(after(blocks[by % ring], *gate), by)
    return [blocks[s] for s in range(ring)]


def shard_kernel(ring, qkv_ref, proj_ref, up_ref, down_ref, *refs):
    out_refs, sem = refs[:-1], refs[-1]
    rows, half = out_refs[0].shape
    side = lax.axis_index("lon") % 2
    start = pl.multiple_of(lax.axis_index("lat") % ring * rows, rows)
    width, hidden = proj_ref.shape[2], up_ref.shape[2]
    split = half - 4 * width

    def run(views):
        copies = []
        for layer, out_ref in enumerate(out_refs):
            at = 0
            for view in views(layer):
                target = out_ref.at[:, pl.ds(at, view.shape[1])]
                copies.append(pltpu.make_async_copy(view, target, sem.at[len(copies)]))
                at += view.shape[1]
        for copy in copies:
            copy.start()
        for copy in copies:
            copy.wait()

    @pl.when(side == 0)
    def _():
        run(
            lambda layer: [qkv_ref.at[layer, i, pl.ds(start, rows), :] for i in range(3)]
            + [proj_ref.at[layer, pl.ds(start, rows), :], up_ref.at[layer, pl.ds(start, rows), pl.ds(0, split)]]
        )

    @pl.when(side == 1)
    def _():
        run(
            lambda layer: [
                up_ref.at[layer, pl.ds(start, rows), pl.ds(split, hidden - split)],
                down_ref.at[layer, pl.ds(start, rows), :],
            ]
        )


def weight_shards(own):
    ring = lat_parts()[1]
    columns = 4 * own[1].shape[2] + 2 * own[2].shape[2]
    shard = jax.ShapeDtypeStruct((own[1].shape[1] // ring, columns // 2), BF)
    return pl.pallas_call(
        partial(shard_kernel, ring),
        out_shape=[shard] * 2,
        in_specs=hbm_specs(4),
        out_specs=vmem_specs(2),
        scratch_shapes=[pltpu.SemaphoreType.DMA((10,))],
        compiler_params=pltpu.CompilerParams(vmem_limit_bytes=58 * 1024 * 1024),
    )(*own)


def pack_kernel(*refs):
    in_refs, out_ref, sem = refs[:-2], refs[-2], refs[-1]
    copies = [pltpu.make_async_copy(ref, out_ref.at[k], sem.at[k]) for k, ref in enumerate(in_refs)]
    for copy in copies:
        copy.start()
    for copy in copies:
        copy.wait()


def pack_shards(fetched):
    return pl.pallas_call(
        pack_kernel,
        out_shape=jax.ShapeDtypeStruct((len(fetched),) + fetched[0].shape, BF),
        in_specs=any_specs(len(fetched)),
        out_specs=pl.BlockSpec(memory_space=pl.ANY),
        scratch_shapes=[pltpu.SemaphoreType.DMA((len(fetched),))],
        compiler_params=pltpu.CompilerParams(vmem_limit_bytes=4 * 1024 * 1024),
        cost_estimate=pl.CostEstimate(flops=1_000_000, bytes_accessed=1_200_000, transcendentals=0),
    )(*fetched)


def load_weights(layer, piece_refs, own_refs, w_ref, sem):
    ring = len(piece_refs) // 2
    rows, half = piece_refs[0].shape[1:]
    core = lax.axis_index("lon") % 2
    place = lax.axis_index("lat") % ring
    copies = []
    at = 0
    for ref in own_refs:
        views = [ref.at[layer, i] for i in range(3)] if len(ref.shape) == 4 else [ref.at[layer]]
        for view in views:
            copies.append((view, w_ref.at[0, :, pl.ds(at, view.shape[1])]))
            at += view.shape[1]
    for s in range(ring):
        start = pl.multiple_of((place - s + ring) % ring * rows, rows)
        for side, ref in ((core, piece_refs[s]), (1 - core, piece_refs[ring + s])):
            columns = pl.ds(pl.multiple_of(side * half, half), half)
            copies.append((ref, w_ref.at[pl.ds(1, PARTS - 1), pl.ds(start, rows), columns]))
    copies = [pltpu.make_async_copy(s, d, sem.at[i]) for i, (s, d) in enumerate(copies)]
    for copy in copies:
        copy.start()
    return copies


class Weights:
    def __init__(self, ref, ends):
        self.ref = ref
        self.ends = ends

    def get(self, k, which):
        return self.ref[k, :, self.ends[which] : self.ends[which + 1]]

    qkv = lambda self, k: self.get(k, 0)
    proj = lambda self, k: self.get(k, 1)
    up = lambda self, k: self.get(k, 2)
    down = lambda self, k: self.get(k, 3)


def head_parts(packed, a):
    width = packed.shape[1] // 3
    return tuple(packed[:, i * width + a * HD : i * width + (a + 1) * HD] for i in range(3))


def forward(x, weights, allowed, packed_ref, probs_ref, mixed_ref, slope_ref):
    normed = norm_rows(x).astype(BF)
    total = jnp.zeros(x.shape, F32)
    for k in range(PARTS):
        packed = dot(normed, weights.qkv(k), 1, 0).astype(BF)
        packed_ref[k] = packed
        count = packed.shape[1] // (3 * HD)
        outs = []
        for a in range(count):
            queries, keys, values = head_parts(packed, a)
            scores = dot(queries, keys, 1, 1) * HD**-0.5
            if allowed is not None:
                scores = jnp.where(allowed, scores, -1e30)
            exps = jnp.exp(scores - jnp.max(scores, axis=-1, keepdims=True))
            probs = exps / jnp.sum(exps, axis=-1, keepdims=True)
            probs_ref[k * count + a] = probs.astype(probs_ref.dtype)
            outs.append(dot(probs.astype(BF), values, 1, 0))
        mixed = jnp.concatenate(outs, axis=1).astype(BF)
        if k == 0:
            mixed_ref[...] = mixed
        total += dot(mixed, weights.proj(k), 1, 1)
    middle = (x + total).astype(BF)
    second = norm_rows(middle.astype(F32)).astype(BF)
    total = jnp.zeros(x.shape, F32)
    for k in range(PARTS):
        active, slope = gelu_and_slope(dot(second, weights.up(k), 1, 0))
        slope_ref[k] = slope.astype(slope_ref.dtype)
        total += dot(active.astype(BF), weights.down(k), 1, 1)
    return middle, (middle.astype(F32) + total).astype(BF)


def core_halves(sums):
    rows, columns = sums.shape
    tiles = sums.reshape(rows // 16, 2, 8, columns)
    even, odd = (
        jnp.concatenate([tiles[:, 0, i : i + 4], tiles[:, 1, i : i + 4]], axis=1).reshape(rows // 2, columns)
        for i in (0, 4)
    )
    here = lax.axis_index("lon") % 2 == 0
    return jnp.where(here, even, odd).astype(BF), jnp.where(here, odd, even).astype(BF)


def backward(x, middle, gradient, weights, factor, packed_ref, probs_ref, mixed_ref, slope_ref, put_sums):
    middle = middle.astype(F32)
    total = jnp.zeros(x.shape, F32)
    for k in range(PARTS):
        d_pre = (slope_ref[k].astype(F32) * dot(gradient, weights.down(k), 1, 0)).astype(BF)
        total += dot(d_pre, weights.up(k), 1, 1)
    mid_grad = (gradient.astype(F32) + norm_pull(middle, total)).astype(BF)
    total = jnp.zeros(x.shape, F32)
    for k in range(PARTS):
        d_mixed = dot(mid_grad, weights.proj(k), 1, 0).astype(BF)
        packed = packed_ref[k]
        width = d_mixed.shape[1]
        count = width // HD
        parts = [[], [], []]
        for a in range(count):
            queries, keys, values = head_parts(packed, a)
            d_out = d_mixed[:, a * HD : (a + 1) * HD]
            probs = probs_ref[k * count + a].astype(F32)
            d_probs = dot(d_out, values, 1, 1)
            d_scores = probs * (d_probs - jnp.sum(d_probs * probs, axis=-1, keepdims=True))
            d_scores = (d_scores * HD**-0.5).astype(BF)
            parts[0].append(dot(d_scores, keys, 1, 0))
            parts[1].append(dot(d_scores, queries, 0, 0))
            parts[2].append(dot(probs.astype(BF), d_out, 0, 0))
        d_packed = jnp.concatenate(parts[0] + parts[1] + parts[2], axis=1).astype(BF)
        total += dot(d_packed, weights.qkv(k), 1, 1)
        if k == 0:
            normed = norm_rows(x).astype(BF)
            first = dot(normed, d_packed, 0, 0) * factor
            second = dot(mid_grad, mixed_ref[...], 0, 0) * factor
            put_sums(jnp.concatenate([first, second], axis=1))
    return (mid_grad.astype(F32) + norm_pull(x, total)).astype(BF)


def first_kernel(pieces, ends, *refs):
    x_ref, refs = refs[0], refs[1:]
    piece_refs, own_refs, refs = refs[:pieces], refs[pieces : pieces + 4], refs[pieces + 4 :]
    out_refs, (middle_ref, *saved), (w_ref, sem) = refs[:PARTS], refs[PARTS:-2], refs[-2:]
    copies = load_weights(0, piece_refs, own_refs, w_ref, sem)
    for copy in copies:
        copy.wait()
    middle, out = forward(x_ref[...].astype(F32), Weights(w_ref, ends), None, *saved)
    middle_ref[...] = middle
    rows = out.shape[0] // PARTS
    for q in range(PARTS):
        out_refs[q][...] = out[q * rows : (q + 1) * rows]


def second_kernel(pieces, ends, factor, *refs):
    x_refs, grad_refs, refs = refs[:PARTS], refs[PARTS : 2 * PARTS], refs[2 * PARTS :]
    mask_ref, *refs = refs
    piece_refs, own_refs, refs = refs[:pieces], refs[pieces : pieces + 4], refs[pieces + 4 :]
    out_refs, (keep_ref, send_ref, w_ref, *saved), sem = refs[:PARTS], refs[PARTS:-1], refs[-1]
    copies = load_weights(1, piece_refs, own_refs, w_ref, sem)
    x = jnp.concatenate([ref[...].astype(F32) for ref in x_refs], axis=0)
    allowed = mask_ref[...] > 0
    for copy in copies:
        copy.wait()
    weights = Weights(w_ref, ends)
    middle, out = forward(x, weights, allowed, *saved)
    rows = out.shape[0] // PARTS
    for q in range(PARTS):
        out_refs[q][0] = out[q * rows : (q + 1) * rows]
    gradient = jnp.concatenate([ref[...].astype(F32) for ref in grad_refs], axis=0).astype(BF)

    def put_sums(value):
        keep_ref[...], send_ref[...] = core_halves(value)

    result = backward(x, middle, gradient, weights, factor, *saved, put_sums)
    for q in range(PARTS):
        out_refs[q][1] = result[q * rows : (q + 1) * rows]


def third_kernel(pieces, ends, factor, *refs):
    grad_refs, (late_keep, late_send, x_ref), refs = refs[:PARTS], refs[PARTS : PARTS + 3], refs[PARTS + 3 :]
    (middle_ref, *saved), refs = refs[:5], refs[5:]
    piece_refs, own_refs, refs = refs[:pieces], refs[pieces : pieces + 4], refs[pieces + 4 :]
    result_ref, keep_ref, send_ref, w_ref, sem = refs
    copies = load_weights(0, piece_refs, own_refs, w_ref, sem)
    gradient = jnp.concatenate([ref[1].astype(F32) for ref in grad_refs], axis=0).astype(BF)
    lats, _, rows, columns = keep_ref.shape
    for late_ref, out_ref in ((late_keep, keep_ref), (late_send, send_ref)):
        out_ref[:, 1] = late_ref[...].reshape(lats, rows, columns)

    def put_sums(value):
        for half, out_ref in zip(core_halves(value), (keep_ref, send_ref)):
            out_ref[:, 0] = half.reshape(lats, rows, columns)

    for copy in copies:
        copy.wait()
    weights = Weights(w_ref, ends)
    result_ref[...] = backward(
        x_ref[...].astype(F32), middle_ref[...], gradient, weights, factor, *saved, put_sums
    )


def vmem_specs(count):
    return [pl.BlockSpec(memory_space=pltpu.VMEM)] * count


def any_specs(count):
    return [pl.BlockSpec(memory_space=pl.ANY)] * count


def hbm_specs(count):
    return [pl.BlockSpec(memory_space=pltpu.HBM)] * count


PARAMS = pltpu.CompilerParams(vmem_limit_bytes=36 * 1024 * 1024)


def cost(flops):
    return pl.CostEstimate(flops=flops, bytes_accessed=8_000_000, transcendentals=600_000)


def scatter(parts, axis, groups=None):
    size = lax.axis_size(axis) if groups is None else len(groups[0])
    parts = parts.reshape(size, -1, parts.shape[-1])
    parts = lax.all_to_all(parts, axis, 0, 0, axis_index_groups=groups)
    return jnp.sum(parts.astype(F32), axis=0)


def per_device(inputs, cotangent, qkv_weight, proj_weight, up_weight, down_weight, shift_labels):
    level_count, lat_rows, lon_cols, model_width = inputs.shape
    head_width = qkv_weight.shape[-1]
    tokens = level_count * lat_rows * lon_cols
    quarter = tokens // PARTS
    factor = float(tokens * lax.axis_size("lat") * lax.axis_size("lon")) ** -0.5

    own = (qkv_weight.swapaxes(1, 2), proj_weight, up_weight, down_weight)
    ends = [0, 3 * head_width, 4 * head_width]
    ends = ends + [ends[-1] + up_weight.shape[2], ends[-1] + 2 * up_weight.shape[2]]
    shards = weight_shards(own)
    early = fetch_heads(shards[0])
    ending = send_quads(list(after(quads(cotangent), shards[0])), 1)
    edge = ((jnp.arange(lat_rows) < 3) & (lax.axis_index("lat") == 0)).astype(jnp.int32)
    region = jnp.broadcast_to((shift_labels * 2 + edge[:, None])[None, :, :, None], (level_count, 6, 12, 1))
    labels = quads(region)[::-1].reshape(-1)
    mask = (labels[:, None] == labels[None, :]).astype(F32)
    start = quads(inputs).reshape(tokens, model_width)
    *early, start, mask, e0, e1, e2, e3 = lax.optimization_barrier((*early, start, mask, *ending))
    ending = (e0, e1, e2, e3)
    early_block = pack_shards(early)
    early_near = ring_near(early_block)
    late = fetch_heads(shards[1], (early_block,))
    early_ring = ring_far(early_near, 1, late[0])
    early_swaps = [swap_cores(early_block)]
    late_block = pack_shards(late)
    late_near = ring_near(late_block, early_ring[2:3], early_ring[1::2])
    early_all = early_ring + early_swaps + [swap_cores(piece) for piece in early_ring[1:]]

    width = head_width // HD * PARTS
    stream = jax.ShapeDtypeStruct((tokens, model_width), BF)
    piece = jax.ShapeDtypeStruct((quarter, model_width), BF)
    pair = jax.ShapeDtypeStruct((2, quarter, model_width), BF)
    sums = jax.ShapeDtypeStruct((model_width // 2, 4 * head_width), BF)
    weight_space = pltpu.VMEM((PARTS, model_width, ends[-1]), BF)
    saved = [
        jax.ShapeDtypeStruct((PARTS, tokens, 3 * head_width), BF),
        jax.ShapeDtypeStruct((width, tokens, tokens), F32),
        jax.ShapeDtypeStruct((tokens, head_width), BF),
        jax.ShapeDtypeStruct((PARTS, tokens, up_weight.shape[2]), F32),
    ]
    held = [jax.ShapeDtypeStruct(s.shape, BF) for s in saved]
    pieces = len(early_all)
    semaphores = pltpu.SemaphoreType.DMA((pieces + 6,))

    *quarters, middle, packed, probs, mixed, slope = pl.pallas_call(
        partial(first_kernel, pieces, ends),
        out_shape=[piece] * PARTS + [stream] + held,
        in_specs=vmem_specs(1) + any_specs(pieces) + hbm_specs(4),
        out_specs=vmem_specs(PARTS + 5),
        scratch_shapes=[weight_space, semaphores],
        compiler_params=PARAMS,
        cost_estimate=cost(1_800_000_000),
    )(start, *early_all, *own)
    late_ring = ring_far(late_near, -1, quarters[0])
    quarters = send_quads(quarters, 1)
    late_swaps = [swap_cores(piece if s == 2 else after(piece, *quarters[1:])) for s, piece in enumerate(late_ring)]
    late_all = late_ring + late_swaps
    *pairs, late_keep, late_send = pl.pallas_call(
        partial(second_kernel, pieces, ends, factor),
        out_shape=[pair] * PARTS + [sums] * 2,
        in_specs=vmem_specs(2 * PARTS + 1) + any_specs(pieces) + hbm_specs(4),
        out_specs=vmem_specs(PARTS + 2),
        scratch_shapes=[weight_space] + [pltpu.VMEM(s.shape, s.dtype) for s in saved] + [semaphores],
        compiler_params=PARAMS,
        cost_estimate=cost(3_800_000_000),
    )(*quarters, *ending, mask, *late_all, *own)
    pairs = send_quads(pairs, -1)
    lats, lons = lax.axis_size("lat"), lax.axis_size("lon")
    both = jax.ShapeDtypeStruct((lats, 2, model_width // lats // 2, 4 * head_width), BF)
    input_grad, keep, send = pl.pallas_call(
        partial(third_kernel, pieces, ends, factor),
        out_shape=[stream, both, both],
        in_specs=vmem_specs(PARTS + 8) + any_specs(pieces) + hbm_specs(4),
        out_specs=vmem_specs(3),
        scratch_shapes=[weight_space, semaphores],
        compiler_params=PARAMS,
        cost_estimate=cost(2_000_000_000),
    )(*pairs, late_keep, late_send, start, middle, packed, probs, mixed, slope, *early_all, *own)

    layer_out = unquads(jnp.stack([p[0] for p in pairs]))
    total = (keep.astype(F32) + swap_cores(send).astype(F32)).astype(BF)
    total = scatter(total, "lat").astype(BF).reshape(2, lons // 2, -1, 4 * head_width).swapaxes(0, 1)
    sides = [list(range(side, lons, 2)) for side in range(2)]
    total = scatter(total, "lon", sides).reshape(2, -1, 4 * head_width)
    pack_sum = total[:, :, : 3 * head_width].reshape(2, -1, 3, head_width)
    proj_sum = total[:, :, 3 * head_width :]
    return layer_out, unquads(input_grad.reshape(PARTS, -1, model_width)), pack_sum, proj_sum


def solution(mesh):
    in_specs = (
        P(None, "lat", "lon", None),
        P(None, "lat", "lon", None),
        P(None, None, None, "head"),
        P(None, None, "head"),
        P(None, None, "head"),
        P(None, None, "head"),
        P("lat", "lon"),
    )
    out_specs = (
        P(None, "lat", "lon", None),
        P(None, "lat", "lon", None),
        P(None, ("lat", "lon"), None, "head"),
        P(None, ("lat", "lon"), "head"),
    )
    return jax.shard_map(
        per_device, mesh=mesh, in_specs=in_specs, out_specs=out_specs, check_vma=False
    )
```

```python
from functools import partial

import jax
import jax.numpy as jnp
import numpy as np
from jax import lax
from jax.experimental import pallas as pl
from jax.experimental.pallas import tpu as pltpu
from jax.sharding import PartitionSpec as P

HD = 64
EPSILON = 1e-05
PARTS = 4
BF = jnp.bfloat16
F32 = jnp.float32


def norm_rows(values):
    average = jnp.mean(values, axis=-1, keepdims=True)
    centred = values - average
    spread = jnp.mean(centred * centred, axis=-1, keepdims=True)
    return centred * lax.rsqrt(spread + EPSILON)


def norm_pull(stream, cotangent):
    stream = stream.astype(F32)
    average = jnp.mean(stream, axis=-1, keepdims=True)
    centred = stream - average
    spread = jnp.mean(centred * centred, axis=-1, keepdims=True)
    inverse = lax.rsqrt(spread + EPSILON)
    unit = centred * inverse
    mean_c = jnp.mean(cotangent, axis=-1, keepdims=True)
    mean_u = jnp.mean(cotangent * unit, axis=-1, keepdims=True)
    return inverse * (cotangent - mean_c - unit * mean_u)


def dot(left, right, left_dim, right_dim):
    return lax.dot_general(
        left, right, (((left_dim,), (right_dim,)), ((), ())), preferred_element_type=F32
    )


def gelu_and_slope(pre):
    cdf = 0.5 * (1.0 + lax.erf(pre * 0.7071067811865476))
    density = jnp.exp(-0.5 * pre * pre) * 0.3989422804014327
    return pre * cdf, cdf + pre * density


def quads(grid):
    channels = grid.shape[-1]
    return (
        grid.reshape(-1, 2, 3, 2, 6, channels).transpose(1, 3, 0, 2, 4, 5).reshape(PARTS, -1, channels)
    )


def unquads(rows):
    channels = rows.shape[-1]
    return (
        rows.reshape(2, 2, -1, 3, 6, channels)
        .transpose(2, 0, 3, 1, 4, 5)
        .reshape(-1, 6, 12, channels)
    )


def joint(sizes, move):
    pairs = []
    for source in np.ndindex(*sizes):
        target = [t % s for t, s in zip(move(*source), sizes)]
        pairs.append((int(np.ravel_multi_index(source, sizes)), int(np.ravel_multi_index(target, sizes))))
    return pairs


def after(value, *others):
    return lax.optimization_barrier((value,) + others)[0]


def send_quads(pieces, sign):
    sizes = (lax.axis_size("lat"), lax.axis_size("lon"))
    out = [pieces[0]]
    for q in (3, 2, 1):
        perm = joint(sizes, lambda a, b: (a + sign * (q // 2), b + sign * (q % 2)))
        out.insert(1, lax.ppermute(pieces[q], ("lat", "lon"), perm))
    return out


def lat_parts():
    lats = lax.axis_size("lat")
    return 2, lats // 2


def fetch_heads(shard, gate=()):
    low, ring = lat_parts()
    sizes = (low * ring, lax.axis_size("head"))
    shard = after(shard, *gate)

    def odd(hops):
        def move(a, h):
            low_now, x = divmod(a, ring)
            return ((1 - low_now) * ring + x, h + (hops if low_now else -hops))

        return joint(sizes, move)

    def even(a, h):
        return (a, h + (1 if a // ring else -1))

    three = lax.ppermute(shard, ("lat", "head"), odd(2))
    two = lax.ppermute(shard, ("lat", "head"), joint(sizes, even))
    one = lax.ppermute(shard, ("lat", "head"), odd(1))
    return one, two, three


def swap_cores(piece):
    size = lax.axis_size("lon")
    return lax.ppermute(piece, "lon", [(i, i ^ 1) for i in range(size)])


def along_x(block, by):
    ring, size = lat_parts()[1], lax.axis_size("lat")
    return lax.ppermute(block, "lat", [(i, i // ring * ring + (i + by) % ring) for i in range(size)])


def ring_near(own, ahead=(), behind=()):
    ring = lat_parts()[1]
    blocks = {0: own, 1 % ring: along_x(after(own, *ahead), 1)}
    if ring > 2:
        blocks[ring - 1] = along_x(after(own, *behind), -1)
    return blocks


def ring_far(blocks, by, *gate):
    ring = lat_parts()[1]
    if ring > 2:
        blocks[2] = along_x(after(blocks[by % ring], *gate), by)
    return [blocks[s] for s in range(ring)]


def shard_kernel(ring, qkv_ref, proj_ref, up_ref, down_ref, *refs):
    out_refs, sem = refs[:-1], refs[-1]
    rows, half = out_refs[0].shape
    side = lax.axis_index("lon") % 2
    start = pl.multiple_of(lax.axis_index("lat") % ring * rows, rows)
    width, hidden = proj_ref.shape[2], up_ref.shape[2]
    split = half - 4 * width

    def run(views):
        copies = []
        for layer, out_ref in enumerate(out_refs):
            at = 0
            for view in views(layer):
                target = out_ref.at[:, pl.ds(at, view.shape[1])]
                copies.append(pltpu.make_async_copy(view, target, sem.at[len(copies)]))
                at += view.shape[1]
        for copy in copies:
            copy.start()
        for copy in copies:
            copy.wait()

    @pl.when(side == 0)
    def _():
        run(
            lambda layer: [qkv_ref.at[layer, i, pl.ds(start, rows), :] for i in range(3)]
            + [proj_ref.at[layer, pl.ds(start, rows), :], up_ref.at[layer, pl.ds(start, rows), pl.ds(0, split)]]
        )

    @pl.when(side == 1)
    def _():
        run(
            lambda layer: [
                up_ref.at[layer, pl.ds(start, rows), pl.ds(split, hidden - split)],
                down_ref.at[layer, pl.ds(start, rows), :],
            ]
        )


def weight_shards(own):
    ring = lat_parts()[1]
    columns = 4 * own[1].shape[2] + 2 * own[2].shape[2]
    shard = jax.ShapeDtypeStruct((own[1].shape[1] // ring, columns // 2), BF)
    return pl.pallas_call(
        partial(shard_kernel, ring),
        out_shape=[shard] * 2,
        in_specs=hbm_specs(4),
        out_specs=vmem_specs(2),
        scratch_shapes=[pltpu.SemaphoreType.DMA((10,))],
        compiler_params=pltpu.CompilerParams(vmem_limit_bytes=58 * 1024 * 1024),
    )(*own)


def pack_kernel(*refs):
    in_refs, out_ref, sem = refs[:-2], refs[-2], refs[-1]
    copies = [pltpu.make_async_copy(ref, out_ref.at[k], sem.at[k]) for k, ref in enumerate(in_refs)]
    for copy in copies:
        copy.start()
    for copy in copies:
        copy.wait()


def pack_shards(fetched):
    return pl.pallas_call(
        pack_kernel,
        out_shape=jax.ShapeDtypeStruct((len(fetched),) + fetched[0].shape, BF),
        in_specs=any_specs(len(fetched)),
        out_specs=pl.BlockSpec(memory_space=pl.ANY),
        scratch_shapes=[pltpu.SemaphoreType.DMA((len(fetched),))],
        compiler_params=pltpu.CompilerParams(vmem_limit_bytes=4 * 1024 * 1024),
        cost_estimate=pl.CostEstimate(flops=1_000_000, bytes_accessed=1_200_000, transcendentals=0),
    )(*fetched)


def load_weights(layer, piece_refs, own_refs, w_ref, sem):
    ring = len(piece_refs) // 2
    rows, half = piece_refs[0].shape[1:]
    core = lax.axis_index("lon") % 2
    place = lax.axis_index("lat") % ring
    copies = []
    at = 0
    for ref in own_refs:
        views = [ref.at[layer, i] for i in range(3)] if len(ref.shape) == 4 else [ref.at[layer]]
        for view in views:
            copies.append((view, w_ref.at[0, :, pl.ds(at, view.shape[1])]))
            at += view.shape[1]
    for s in range(ring):
        start = pl.multiple_of((place - s + ring) % ring * rows, rows)
        for side, ref in ((core, piece_refs[s]), (1 - core, piece_refs[ring + s])):
            columns = pl.ds(pl.multiple_of(side * half, half), half)
            copies.append((ref, w_ref.at[pl.ds(1, PARTS - 1), pl.ds(start, rows), columns]))
    copies = [pltpu.make_async_copy(s, d, sem.at[i]) for i, (s, d) in enumerate(copies)]
    for copy in copies:
        copy.start()
    return copies


class Weights:
    def __init__(self, ref, ends):
        self.ref = ref
        self.ends = ends

    def get(self, k, which):
        return self.ref[k, :, self.ends[which] : self.ends[which + 1]]

    qkv = lambda self, k: self.get(k, 0)
    proj = lambda self, k: self.get(k, 1)
    up = lambda self, k: self.get(k, 2)
    down = lambda self, k: self.get(k, 3)


def head_parts(packed, a):
    width = packed.shape[1] // 3
    return tuple(packed[:, i * width + a * HD : i * width + (a + 1) * HD] for i in range(3))


def forward(x, weights, allowed, packed_ref, probs_ref, mixed_ref, slope_ref):
    normed = norm_rows(x).astype(BF)
    total = jnp.zeros(x.shape, F32)
    for k in range(PARTS):
        packed = dot(normed, weights.qkv(k), 1, 0).astype(BF)
        packed_ref[k] = packed
        count = packed.shape[1] // (3 * HD)
        outs = []
        for a in range(count):
            queries, keys, values = head_parts(packed, a)
            scores = dot(queries, keys, 1, 1) * HD**-0.5
            if allowed is not None:
                scores = jnp.where(allowed, scores, -1e30)
            exps = jnp.exp(scores - jnp.max(scores, axis=-1, keepdims=True))
            probs = exps / jnp.sum(exps, axis=-1, keepdims=True)
            probs_ref[k * count + a] = probs.astype(probs_ref.dtype)
            outs.append(dot(probs.astype(BF), values, 1, 0))
        mixed = jnp.concatenate(outs, axis=1).astype(BF)
        if k == 0:
            mixed_ref[...] = mixed
        total += dot(mixed, weights.proj(k), 1, 1)
    middle = (x + total).astype(BF)
    second = norm_rows(middle.astype(F32)).astype(BF)
    total = jnp.zeros(x.shape, F32)
    for k in range(PARTS):
        active, slope = gelu_and_slope(dot(second, weights.up(k), 1, 0))
        slope_ref[k] = slope.astype(slope_ref.dtype)
        total += dot(active.astype(BF), weights.down(k), 1, 1)
    return middle, (middle.astype(F32) + total).astype(BF)


def core_halves(sums):
    rows, columns = sums.shape
    tiles = sums.reshape(rows // 16, 2, 8, columns)
    even, odd = (
        jnp.concatenate([tiles[:, 0, i : i + 4], tiles[:, 1, i : i + 4]], axis=1).reshape(rows // 2, columns)
        for i in (0, 4)
    )
    here = lax.axis_index("lon") % 2 == 0
    return jnp.where(here, even, odd).astype(BF), jnp.where(here, odd, even).astype(BF)


def backward(x, middle, gradient, weights, factor, packed_ref, probs_ref, mixed_ref, slope_ref, put_sums):
    middle = middle.astype(F32)
    total = jnp.zeros(x.shape, F32)
    for k in range(PARTS):
        d_pre = (slope_ref[k].astype(F32) * dot(gradient, weights.down(k), 1, 0)).astype(BF)
        total += dot(d_pre, weights.up(k), 1, 1)
    mid_grad = (gradient.astype(F32) + norm_pull(middle, total)).astype(BF)
    total = jnp.zeros(x.shape, F32)
    for k in range(PARTS):
        d_mixed = dot(mid_grad, weights.proj(k), 1, 0).astype(BF)
        packed = packed_ref[k]
        width = d_mixed.shape[1]
        count = width // HD
        parts = [[], [], []]
        for a in range(count):
            queries, keys, values = head_parts(packed, a)
            d_out = d_mixed[:, a * HD : (a + 1) * HD]
            probs = probs_ref[k * count + a].astype(F32)
            d_probs = dot(d_out, values, 1, 1)
            d_scores = probs * (d_probs - jnp.sum(d_probs * probs, axis=-1, keepdims=True))
            d_scores = (d_scores * HD**-0.5).astype(BF)
            parts[0].append(dot(d_scores, keys, 1, 0))
            parts[1].append(dot(d_scores, queries, 0, 0))
            parts[2].append(dot(probs.astype(BF), d_out, 0, 0))
        d_packed = jnp.concatenate(parts[0] + parts[1] + parts[2], axis=1).astype(BF)
        total += dot(d_packed, weights.qkv(k), 1, 1)
        if k == 0:
            normed = norm_rows(x).astype(BF)
            first = dot(normed, d_packed, 0, 0) * factor
            second = dot(mid_grad, mixed_ref[...], 0, 0) * factor
            put_sums(jnp.concatenate([first, second], axis=1))
    return (mid_grad.astype(F32) + norm_pull(x, total)).astype(BF)


def first_kernel(pieces, ends, *refs):
    x_ref, refs = refs[0], refs[1:]
    piece_refs, own_refs, refs = refs[:pieces], refs[pieces : pieces + 4], refs[pieces + 4 :]
    out_refs, (middle_ref, *saved), (w_ref, sem) = refs[:PARTS], refs[PARTS:-2], refs[-2:]
    copies = load_weights(0, piece_refs, own_refs, w_ref, sem)
    for copy in copies:
        copy.wait()
    middle, out = forward(x_ref[...].astype(F32), Weights(w_ref, ends), None, *saved)
    middle_ref[...] = middle
    rows = out.shape[0] // PARTS
    for q in range(PARTS):
        out_refs[q][...] = out[q * rows : (q + 1) * rows]


def second_kernel(pieces, ends, factor, *refs):
    x_refs, grad_refs, refs = refs[:PARTS], refs[PARTS : 2 * PARTS], refs[2 * PARTS :]
    mask_ref, *refs = refs
    piece_refs, own_refs, refs = refs[:pieces], refs[pieces : pieces + 4], refs[pieces + 4 :]
    out_refs, (keep_ref, send_ref, w_ref, *saved), sem = refs[:PARTS], refs[PARTS:-1], refs[-1]
    copies = load_weights(1, piece_refs, own_refs, w_ref, sem)
    x = jnp.concatenate([ref[...].astype(F32) for ref in x_refs], axis=0)
    allowed = mask_ref[...] > 0
    for copy in copies:
        copy.wait()
    weights = Weights(w_ref, ends)
    middle, out = forward(x, weights, allowed, *saved)
    rows = out.shape[0] // PARTS
    for q in range(PARTS):
        out_refs[q][0] = out[q * rows : (q + 1) * rows]
    gradient = jnp.concatenate([ref[...].astype(F32) for ref in grad_refs], axis=0).astype(BF)

    def put_sums(value):
        keep_ref[...], send_ref[...] = core_halves(value)

    result = backward(x, middle, gradient, weights, factor, *saved, put_sums)
    for q in range(PARTS):
        out_refs[q][1] = result[q * rows : (q + 1) * rows]


def third_kernel(pieces, ends, factor, *refs):
    grad_refs, (late_keep, late_send, x_ref), refs = refs[:PARTS], refs[PARTS : PARTS + 3], refs[PARTS + 3 :]
    (middle_ref, *saved), refs = refs[:5], refs[5:]
    piece_refs, own_refs, refs = refs[:pieces], refs[pieces : pieces + 4], refs[pieces + 4 :]
    result_ref, keep_ref, send_ref, w_ref, sem = refs
    copies = load_weights(0, piece_refs, own_refs, w_ref, sem)
    gradient = jnp.concatenate([ref[1].astype(F32) for ref in grad_refs], axis=0).astype(BF)
    lats, _, rows, columns = keep_ref.shape
    for late_ref, out_ref in ((late_keep, keep_ref), (late_send, send_ref)):
        out_ref[:, 1] = late_ref[...].reshape(lats, rows, columns)

    def put_sums(value):
        for half, out_ref in zip(core_halves(value), (keep_ref, send_ref)):
            out_ref[:, 0] = half.reshape(lats, rows, columns)

    for copy in copies:
        copy.wait()
    weights = Weights(w_ref, ends)
    result_ref[...] = backward(
        x_ref[...].astype(F32), middle_ref[...], gradient, weights, factor, *saved, put_sums
    )


def vmem_specs(count):
    return [pl.BlockSpec(memory_space=pltpu.VMEM)] * count


def any_specs(count):
    return [pl.BlockSpec(memory_space=pl.ANY)] * count


def hbm_specs(count):
    return [pl.BlockSpec(memory_space=pltpu.HBM)] * count


PARAMS = pltpu.CompilerParams(vmem_limit_bytes=36 * 1024 * 1024)


def cost(flops):
    return pl.CostEstimate(flops=flops, bytes_accessed=8_000_000, transcendentals=600_000)


def scatter(parts, axis, groups=None):
    size = lax.axis_size(axis) if groups is None else len(groups[0])
    parts = parts.reshape(size, -1, parts.shape[-1])
    parts = lax.all_to_all(parts, axis, 0, 0, axis_index_groups=groups)
    return jnp.sum(parts.astype(F32), axis=0)


def per_device(inputs, cotangent, qkv_weight, proj_weight, up_weight, down_weight, shift_labels):
    level_count, lat_rows, lon_cols, model_width = inputs.shape
    head_width = qkv_weight.shape[-1]
    tokens = level_count * lat_rows * lon_cols
    quarter = tokens // PARTS
    factor = float(tokens * lax.axis_size("lat") * lax.axis_size("lon")) ** -0.5

    own = (qkv_weight.swapaxes(1, 2), proj_weight, up_weight, down_weight)
    ends = [0, 3 * head_width, 4 * head_width]
    ends = ends + [ends[-1] + up_weight.shape[2], ends[-1] + 2 * up_weight.shape[2]]
    shards = weight_shards(own)
    early = fetch_heads(shards[0])
    late = fetch_heads(shards[1])
    ending = send_quads(list(after(quads(cotangent), shards[0])), 1)
    edge = ((jnp.arange(lat_rows) < 3) & (lax.axis_index("lat") == 0)).astype(jnp.int32)
    region = jnp.broadcast_to((shift_labels * 2 + edge[:, None])[None, :, :, None], (level_count, 6, 12, 1))
    labels = quads(region)[::-1].reshape(-1)
    mask = (labels[:, None] == labels[None, :]).astype(F32)
    start = quads(inputs).reshape(tokens, model_width)
    *early, start, mask, e0, e1, e2, e3 = lax.optimization_barrier((*early, start, mask, *ending))
    ending = (e0, e1, e2, e3)
    early_block = pack_shards(early)
    early_near = ring_near(early_block)
    early_ring = ring_far(early_near, 1)
    held = [piece if s in (0, 1, 2, 3) else after(piece, early_ring[2]) for s, piece in enumerate(early_ring)]
    early_swaps = [swap_cores(piece) for piece in held]
    early_all = early_ring + early_swaps
    late_block = pack_shards(lax.optimization_barrier((*late, early_ring[1], early_ring[-1]))[:3])
    late_near = ring_near(late_block, early_ring[2:3])
    late_own = swap_cores(late_block)
    start = after(start, late_own)

    width = head_width // HD * PARTS
    stream = jax.ShapeDtypeStruct((tokens, model_width), BF)
    piece = jax.ShapeDtypeStruct((quarter, model_width), BF)
    pair = jax.ShapeDtypeStruct((2, quarter, model_width), BF)
    sums = jax.ShapeDtypeStruct((model_width // 2, 4 * head_width), BF)
    weight_space = pltpu.VMEM((PARTS, model_width, ends[-1]), BF)
    saved = [
        jax.ShapeDtypeStruct((PARTS, tokens, 3 * head_width), BF),
        jax.ShapeDtypeStruct((width, tokens, tokens), F32),
        jax.ShapeDtypeStruct((tokens, head_width), BF),
        jax.ShapeDtypeStruct((PARTS, tokens, up_weight.shape[2]), F32),
    ]
    held = [jax.ShapeDtypeStruct(s.shape, BF) for s in saved]
    pieces = len(early_all)
    semaphores = pltpu.SemaphoreType.DMA((pieces + 6,))

    *quarters, middle, packed, probs, mixed, slope = pl.pallas_call(
        partial(first_kernel, pieces, ends),
        out_shape=[piece] * PARTS + [stream] + held,
        in_specs=vmem_specs(1) + any_specs(pieces) + hbm_specs(4),
        out_specs=vmem_specs(PARTS + 5),
        scratch_shapes=[weight_space, semaphores],
        compiler_params=PARAMS,
        cost_estimate=cost(1_800_000_000),
    )(start, *early_all, *own)
    late_ring = ring_far(late_near, -1, late_own)
    quarters = send_quads(quarters, 1)
    late_all = late_ring + [late_own] + [swap_cores(after(p, *quarters[1:]) if s != 1 else p) for s, p in enumerate(late_ring[1:])]
    *pairs, late_keep, late_send = pl.pallas_call(
        partial(second_kernel, pieces, ends, factor),
        out_shape=[pair] * PARTS + [sums] * 2,
        in_specs=vmem_specs(2 * PARTS + 1) + any_specs(pieces) + hbm_specs(4),
        out_specs=vmem_specs(PARTS + 2),
        scratch_shapes=[weight_space] + [pltpu.VMEM(s.shape, s.dtype) for s in saved] + [semaphores],
        compiler_params=PARAMS,
        cost_estimate=cost(3_800_000_000),
    )(*quarters, *ending, mask, *late_all, *own)
    pairs = send_quads(pairs, -1)
    lats, lons = lax.axis_size("lat"), lax.axis_size("lon")
    both = jax.ShapeDtypeStruct((lats, 2, model_width // lats // 2, 4 * head_width), BF)
    input_grad, keep, send = pl.pallas_call(
        partial(third_kernel, pieces, ends, factor),
        out_shape=[stream, both, both],
        in_specs=vmem_specs(PARTS + 8) + any_specs(pieces) + hbm_specs(4),
        out_specs=vmem_specs(3),
        scratch_shapes=[weight_space, semaphores],
        compiler_params=PARAMS,
        cost_estimate=cost(2_000_000_000),
    )(*pairs, late_keep, late_send, start, middle, packed, probs, mixed, slope, *early_all, *own)

    layer_out = unquads(jnp.stack([p[0] for p in pairs]))
    total = (keep.astype(F32) + swap_cores(send).astype(F32)).astype(BF)
    total = scatter(total, "lat").astype(BF).reshape(2, lons // 2, -1, 4 * head_width).swapaxes(0, 1)
    sides = [list(range(side, lons, 2)) for side in range(2)]
    total = scatter(total, "lon", sides).reshape(2, -1, 4 * head_width)
    pack_sum = total[:, :, : 3 * head_width].reshape(2, -1, 3, head_width)
    proj_sum = total[:, :, 3 * head_width :]
    return layer_out, unquads(input_grad.reshape(PARTS, -1, model_width)), pack_sum, proj_sum


def solution(mesh):
    in_specs = (
        P(None, "lat", "lon", None),
        P(None, "lat", "lon", None),
        P(None, None, None, "head"),
        P(None, None, "head"),
        P(None, None, "head"),
        P(None, None, "head"),
        P("lat", "lon"),
    )
    out_specs = (
        P(None, "lat", "lon", None),
        P(None, "lat", "lon", None),
        P(None, ("lat", "lon"), None, "head"),
        P(None, ("lat", "lon"), "head"),
    )
    return jax.shard_map(
        per_device, mesh=mesh, in_specs=in_specs, out_specs=out_specs, check_vma=False
    )
```
